32 devices in a mesh: subj: 4 (over z), vox: 8 (over y, x, core).
Axes of the slice: x: 2, y: 2, z: 4, core: 2. Of those that a mesh axis runs over, the one named last changes fastest.
Arguments:
- features: bfloat16 [4096, 4096], P(('subj', 'vox')), may hold values from -20 to 20
- token_ticks: int32 [4096], replicated, may hold values from 0 to 24575, as said below
- offsets: int32 [4], P('subj'), may hold values from 0 to 63
- run_lengths: int32 [4, 8], P('subj'), may hold values from 1 to 128, 384 in all within a row
- penalty: float32 [4], P('subj'), may hold values from 0.05 to 0.5
- responses: float32 [4, 384, 1024], P('subj', None, 'vox'), may hold values from -6 to 6
Outputs:
- weights: bfloat16 [4, 4, 4096, 1024], P('subj', None, 'vox')
The draws below stay inside these ranges and needn't reach their ends.
Inputs may be any that keep to these rules, and one draw needn't show every extreme that they name: `token_ticks`: token k's tick lies between k * 6 and k * 6 + 5. `run_lengths`: each subject's 8 runs together cover its 384 TRs in order.
All inputs are finite; a program needn't handle non-finite values.
Results may differ from the reference program's by a relative error of at most 0.023.
The reference program's roundings to bfloat16 on the way count: a program that leaves them out, or rounds other values in their place, can miss the bound.
Values may be sent and summed in bfloat16 or wider, within the bound.
A program may use at most 128 MiB of HBM per device.

```python
import math
import jax
import jax.numpy as jnp
import numpy as np
from jax import lax

F = 4096
DELAYS = 4
TICKS = 64
GAP = 6
RUNS = 8
SUBJECTS = 4
TOKENS = 4096
TR_ALL = 384
VOXELS = 1024


def draw_features(key, part):
    key = jax.random.fold_in(key, 11)
    first_key, second_key, third_key, fourth_key, fifth_key, sixth_key = jax.random.split(key, 6)
    latent_rank = 256
    block_tokens = 8
    amplitude = np.floor(2048.0 * 10.0 ** (-3.0 * np.arange(latent_rank) / latent_rank))
    latent_norm = float(np.sqrt(np.sum(amplitude * amplitude) * (15.0 * 15.0 - 1.0) / 12.0))
    block_count = (TOKENS + block_tokens - 1) // block_tokens
    levels = jax.random.randint(first_key, (block_count, latent_rank), -7, 8, jnp.int32).astype(jnp.float32)
    levels = levels * jnp.asarray(amplitude, jnp.float32)[None, :]
    signs = (jax.random.randint(second_key, (latent_rank, F), 0, 2, jnp.int32) * 2 - 1).astype(jnp.float32)
    latent = jnp.dot(levels, signs, precision=lax.Precision.HIGHEST)
    latent = jnp.repeat(latent, block_tokens, axis=0)[:TOKENS] / latent_norm
    column_scale = jnp.exp(jax.random.uniform(third_key, (1, F), jnp.float32) * math.log(10.0)) / 4.64
    row_scale = jnp.exp(jax.random.uniform(fourth_key, (TOKENS, 1), jnp.float32) * math.log(10.0)) / 4.64
    noise = jnp.clip(jax.random.normal(fifth_key, (TOKENS, F), jnp.float32), -4.0, 4.0) * 0.85
    shared_part = jnp.clip(jax.random.normal(sixth_key, (1, F), jnp.float32) * 0.3, -1.0, 1.0)
    values = latent * 1.6 + noise + shared_part
    return jnp.clip(values * row_scale * column_scale, -20.0, 20.0).astype(jnp.bfloat16)


def draw_token_ticks(key, part):
    key = jax.random.fold_in(key, 5)
    jitter = jax.random.randint(key, (TOKENS,), 0, GAP, jnp.int32)
    jitter = jitter.at[0].set(0).at[TOKENS - 1].set(GAP - 1)
    return jnp.arange(TOKENS, dtype=jnp.int32) * GAP + jitter


def plant(entries, stream_key, least, high):
    longest = entries.shape.index(max(entries.shape))
    spots = []
    for shift in (0, 1):
        where = [jax.random.randint(jax.random.fold_in(stream_key, axis), (), 0, length) for axis, length in enumerate(entries.shape)]
        where[longest] = (where[longest] + shift) % entries.shape[longest]
        spots.append(tuple(where))
    return entries.at[spots[0]].set(least).at[spots[1]].set(high)


def level_of(own_key, dims, shards, least, top_value):
    def one(position, parts):
        heights = jax.random.uniform(jax.random.fold_in(jax.random.fold_in(own_key, 6), position), (parts,), jnp.float32, least / len(shards), top_value / len(shards))
        return jnp.repeat(jnp.exp(heights), dims[position] // parts).reshape((-1,) + (1,) * (len(dims) - position - 1))

    level = one(*shards[0])
    for cut in shards[1:]:
        level = level * one(*cut)
    return level


def length_profile(number_of, total, most, skew):
    weights = [(1 << 20) // math.isqrt(rank ** skew) + 1 for rank in range(2, number_of + 1)]
    surplus, holding = total - most - (number_of - 1), [1] * (number_of - 1)
    while surplus > 0:
        free = [i for i in range(number_of - 1) if holding[i] < most]
        whole, left = sum([weights[i] for i in free]), surplus
        for i in free:
            addition = min(most - holding[i], max(1, left * weights[i] // whole), surplus)
            holding[i] = holding[i] + addition
            surplus = surplus - addition
    return np.array([most] + holding)


def ragged(stream_key, count, total, bound, slope):
    if count == 2:
        one = jax.random.randint(stream_key, (), max(1, total - bound), min(bound, total - 1) + 1)
        return jnp.stack([one, total - one])
    tallies = jnp.asarray(length_profile(count, total, bound, slope), jnp.int32)
    pairs = (count - 1) // 2
    giver, taker = tallies[1:1 + 2 * pairs:2], tallies[2:2 + 2 * pairs:2]
    slack = jnp.minimum(giver - 1, bound - taker)
    passed = jax.random.randint(jax.random.fold_in(stream_key, 1), (pairs,), 0, 1 << 20) % (slack + 1)
    tallies = tallies.at[1:1 + 2 * pairs:2].set(giver - passed).at[2:2 + 2 * pairs:2].set(taker + passed)
    return tallies[jax.random.permutation(jax.random.fold_in(stream_key, 2), count)]


def bell_draw(key, dims, scale, limit, cuts=(), held_as=jnp.bfloat16):
    result = scale * jax.random.normal(key, dims, jnp.float32)
    if cuts:
        result = result * level_of(key, dims, cuts, -0.22, 0.18)
    return jnp.clip(result, -limit, limit).astype(held_as)


def setup_inputs(seed: int = 0) -> dict:
    key_list = jax.random.split(jax.random.key(seed), 7)
    features = draw_features(jax.random.fold_in(key_list[6], 71), 0)
    token_ticks = draw_token_ticks(jax.random.fold_in(key_list[6], 71), 0)
    offsets = plant(jax.random.randint(key_list[2], (SUBJECTS,), 0, TICKS), jax.random.fold_in(key_list[2], 1), 0, TICKS - 1).astype(jnp.int32)
    run_lengths = jax.vmap(lambda own: ragged(own, RUNS, TR_ALL, TR_ALL // 3, 1))(jax.random.split(key_list[3], SUBJECTS)).reshape((SUBJECTS, RUNS)).astype(jnp.int32)
    penalty = jnp.clip(jnp.exp(math.log(0.5) - 2.3025851 * jax.random.uniform(key_list[4], (SUBJECTS,), jnp.float32) ** level_of(key_list[4], (SUBJECTS,), ((0, 4),), -0.2, 0.2)), 0.05, 0.5)
    responses = bell_draw(key_list[5], (SUBJECTS, TR_ALL, VOXELS), 1.0, 6.0, ((0, 4), (2, 8)), jnp.float32)
    return dict(features=features, token_ticks=token_ticks, offsets=offsets, run_lengths=run_lengths, penalty=penalty, responses=responses)


def lanczos_table(token_ticks, offset, tr_rows):
    distance = token_ticks[None, :] - (tr_rows[:, None] * TICKS + offset)
    inside = jnp.abs(distance) < 3 * TICKS
    scaled = distance.astype(jnp.float32) / TICKS
    shaped = jnp.sinc(scaled) * jnp.sinc(scaled / 3.0)
    return jnp.where(inside, shaped, jnp.zeros_like(shaped)).astype(jnp.bfloat16)

def delay_stack(interp, lengths, tr_total):
    starts = jnp.cumsum(lengths) - lengths
    tr_steps = jnp.arange(tr_total, dtype=jnp.int32)
    run_first = jnp.max(jnp.where(starts[None, :] <= tr_steps[:, None], starts[None, :], 0), axis=1)
    delayed = []
    for delay_step in range(1, DELAYS + 1):
        moved = jnp.concatenate([jnp.zeros((delay_step, interp.shape[1]), interp.dtype), interp[:-delay_step]], axis=0)
        keep_rows = (tr_steps - delay_step >= run_first)[:, None]
        delayed.append(jnp.where(keep_rows, moved, jnp.zeros_like(moved)))
    return jnp.stack(delayed, axis=1)

def reference(features, token_ticks, offsets, run_lengths, penalty, responses):
    features_wide = features.astype(jnp.float32)
    tr_rows = jnp.arange(TR_ALL, dtype=jnp.int32)
    spread = (GAP / TICKS) ** 0.5

    def one_subject(inputs):
        offset, lengths, ridge, targets = inputs
        weights_table = lanczos_table(token_ticks, offset, tr_rows).astype(jnp.float32)
        summed = jnp.dot(weights_table, features_wide, precision=lax.Precision.HIGHEST)
        interp = (summed * spread).astype(jnp.bfloat16)
        stacked = delay_stack(interp, lengths, TR_ALL).reshape(TR_ALL, DELAYS * F).astype(jnp.float32)
        kernel = jnp.dot(stacked, stacked.T, precision=lax.Precision.HIGHEST) / (DELAYS * F)
        system = kernel + ridge * jnp.eye(TR_ALL, dtype=jnp.float32)
        factor = jnp.linalg.cholesky(system)
        forward = lax.linalg.triangular_solve(factor, targets, left_side=True, lower=True)
        dual_coef = lax.linalg.triangular_solve(factor, forward, left_side=True, lower=True, transpose_a=True).astype(jnp.bfloat16)
        projected = jnp.dot(stacked.T, dual_coef.astype(jnp.float32), precision=lax.Precision.HIGHEST)
        projected = projected * (DELAYS * F) ** (-0.5)
        return projected.reshape(DELAYS, F, VOXELS).astype(jnp.bfloat16)
    return lax.map(one_subject, (offsets, run_lengths, penalty, responses))
```

```python
import functools

import jax
import jax.numpy as jnp
from jax import lax
from jax.experimental import pallas as pl
from jax.experimental.pallas import tpu as pltpu
from jax.sharding import PartitionSpec as P

DELAYS = 4
TICKS = 64
GAP = 6
BLOCK = 128
AXES = ("subj", "vox")
FULL = lax.Precision.HIGHEST
MESH = pl.DeviceIdType.MESH


def lanczos_rows(near_ticks, offset, tr_rows):
    distance = near_ticks[None, :] - (tr_rows[:, None] * TICKS + offset)
    inside = jnp.abs(distance) < 3 * TICKS
    scaled = distance.astype(jnp.float32) / TICKS
    shaped = jnp.sinc(scaled) * jnp.sinc(scaled / 3.0)
    return jnp.where(inside, shaped, jnp.zeros_like(shaped)).astype(jnp.bfloat16)


def delay_stack(interp, lengths, tr_total):
    starts = jnp.cumsum(lengths) - lengths
    tr_steps = jnp.arange(tr_total, dtype=jnp.int32)
    run_first = jnp.max(jnp.where(starts[None, :] <= tr_steps[:, None], starts[None, :], 0), axis=1)
    delayed = []
    for delay_step in range(1, DELAYS + 1):
        moved = jnp.concatenate(
            [jnp.zeros((delay_step, interp.shape[1]), interp.dtype), interp[:-delay_step]], axis=0
        )
        keep_rows = (tr_steps - delay_step >= run_first)[:, None]
        delayed.append(jnp.where(keep_rows, moved, jnp.zeros_like(moved)))
    return jnp.concatenate(delayed, axis=1)


def gram_kernel(n, scale, stacked_ref, out_ref, part, land, send_a, recv_a, send_b, recv_b):
    me = lax.axis_index("vox")
    total = out_ref.shape[0]
    rows = total // n
    barrier = pltpu.get_barrier_semaphore()
    for step in range(1, n):
        pl.semaphore_signal(
            barrier, inc=1, device_id={"vox": lax.rem(me + step, n)}, device_id_type=MESH
        )

    @pl.loop(0, total // BLOCK)
    def _(block):
        here = pl.ds(pl.multiple_of(block * BLOCK, BLOCK), BLOCK)
        part[here, :] = lax.dot_general(
            stacked_ref[here, :], stacked_ref[...], (((1,), (1,)), ((), ())),
            preferred_element_type=jnp.float32,
        )

    pl.semaphore_wait(barrier, n - 1)

    def rows_of(owner):
        return pl.ds(pl.multiple_of(owner * rows, rows), rows)

    def share(step):
        peer = lax.rem(me + step, n)
        return pltpu.make_async_remote_copy(
            src_ref=part.at[rows_of(peer), :], dst_ref=land.at[me],
            send_sem=send_a.at[step], recv_sem=recv_a.at[me],
            device_id={"vox": peer}, device_id_type=MESH,
        )

    def arrived(step):
        peer = lax.rem(me + step, n)
        return pltpu.make_async_remote_copy(
            src_ref=part.at[rows_of(me), :], dst_ref=land.at[peer],
            send_sem=send_a.at[step], recv_sem=recv_a.at[peer],
            device_id={"vox": peer}, device_id_type=MESH,
        )

    def spread(step):
        peer = lax.rem(me + step, n)
        return pltpu.make_async_remote_copy(
            src_ref=out_ref.at[rows_of(me), :], dst_ref=out_ref.at[rows_of(me), :],
            send_sem=send_b.at[step], recv_sem=recv_b.at[me],
            device_id={"vox": peer}, device_id_type=MESH,
        )

    def spread_in(step):
        peer = lax.rem(me + step, n)
        return pltpu.make_async_remote_copy(
            src_ref=out_ref.at[rows_of(peer), :], dst_ref=out_ref.at[rows_of(peer), :],
            send_sem=send_b.at[step], recv_sem=recv_b.at[peer],
            device_id={"vox": peer}, device_id_type=MESH,
        )

    for step in range(1, n):
        share(step).start()
    total_rows = part[rows_of(me), :]
    for step in range(1, n):
        arrived(step).wait_recv()
        total_rows = total_rows + land[lax.rem(me + step, n)]
    out_ref[rows_of(me), :] = total_rows * scale
    for step in range(1, n):
        spread(step).start()
    for step in range(1, n):
        spread_in(step).wait_recv()
    for step in range(1, n):
        share(step).wait_send()
        spread(step).wait_send()


def gram_sum(stacked, n, width):
    total = stacked.shape[0]
    rows = total // n
    return pl.pallas_call(
        functools.partial(gram_kernel, n, 1.0 / (DELAYS * width)),
        out_shape=jax.ShapeDtypeStruct((total, total), jnp.float32),
        in_specs=[pl.BlockSpec(memory_space=pltpu.VMEM)],
        out_specs=pl.BlockSpec(memory_space=pltpu.VMEM),
        scratch_shapes=[
            pltpu.VMEM((total, total), jnp.float32),
            pltpu.VMEM((n, rows, total), jnp.float32),
            pltpu.SemaphoreType.DMA((n,)),
            pltpu.SemaphoreType.DMA((n,)),
            pltpu.SemaphoreType.DMA((n,)),
            pltpu.SemaphoreType.DMA((n,)),
        ],
        compiler_params=pltpu.CompilerParams(
            collective_id=0, has_side_effects=True, vmem_limit_bytes=48 * 2**20
        ),
        name="gram_sum",
    )(stacked)


def full_dot(a, b):
    return jnp.dot(a, b, precision=FULL, preferred_element_type=jnp.float32)


def solve_kernel(kernel_ref, penalty_ref, targets_ref, out_ref, work, pair):
    total, voxels = targets_ref.shape
    blocks = total // BLOCK
    penalty = penalty_ref[0]
    row = lax.broadcasted_iota(jnp.int32, (BLOCK, BLOCK), 0)
    col = lax.broadcasted_iota(jnp.int32, (BLOCK, BLOCK), 1)
    eye = jnp.where(row == col, 1.0, 0.0).astype(jnp.float32)
    work[:, :total] = kernel_ref[...]
    work[:, total:] = targets_ref[...]
    for k in range(blocks):
        here = slice(k * BLOCK, (k + 1) * BLOCK)
        work[here, here] = work[here, here] + penalty * eye
    low = penalty * 0.9
    for k in range(blocks):
        here = slice(k * BLOCK, (k + 1) * BLOCK)
        after = (k + 1) * BLOCK
        diagonal = work[here, here]
        high = jnp.max(jnp.sum(jnp.abs(diagonal), axis=1))
        first = 2.0 / (low + high)
        pair[:BLOCK] = first * eye
        pair[BLOCK:] = first * diagonal

        def going(least):
            return least < 1.0 - 2.0**-12

        def step(least):
            inner = least * (2.0 - least)
            grow = 2.0 / (1.0 + inner)
            pair[...] = full_dot(pair[...], grow * (2.0 * eye - pair[BLOCK:]))
            return inner * grow

        lax.while_loop(going, step, low * first)
        inverse = pair[:BLOCK]
        inverse = inverse + full_dot(inverse, eye - full_dot(diagonal, inverse))
        ahead = full_dot(inverse, work[here, after:])
        work[here, after:] = ahead
        rest = blocks - 1 - k
        if 0 < rest <= 2:
            work[after:total, after:] -= full_dot(work[after:total, here], ahead)
        elif rest:

            @pl.loop(k + 1, blocks)
            def _(below):
                there = pl.ds(pl.multiple_of(below * BLOCK, BLOCK), BLOCK)
                work[there, after:] -= full_dot(work[there, here], work[here, after:])

    for k in range(blocks - 2, -1, -1):
        here = slice(k * BLOCK, (k + 1) * BLOCK)
        after = (k + 1) * BLOCK
        work[here, total:] -= full_dot(work[here, after:total], work[after:total, total:])
    out_ref[...] = work[:, total:].astype(out_ref.dtype)


def solve(kernel, penalty, targets):
    total, voxels = targets.shape
    return pl.pallas_call(
        solve_kernel,
        out_shape=jax.ShapeDtypeStruct((total, voxels), jnp.bfloat16),
        in_specs=[
            pl.BlockSpec(memory_space=pltpu.VMEM),
            pl.BlockSpec(memory_space=pltpu.SMEM),
            pl.BlockSpec(memory_space=pltpu.VMEM),
        ],
        out_specs=pl.BlockSpec(memory_space=pltpu.VMEM),
        scratch_shapes=[
            pltpu.VMEM((total, total + voxels), jnp.float32),
            pltpu.VMEM((2 * BLOCK, BLOCK), jnp.float32),
        ],
        compiler_params=pltpu.CompilerParams(vmem_limit_bytes=48 * 2**20),
        name="ridge_solve",
    )(kernel, penalty, targets)


def all_offsets(offsets):
    count = lax.axis_size("subj")
    found = [offsets]
    for turn in range(1, count):
        found.append(lax.ppermute(offsets, "subj", [(i, (i + turn) % count) for i in range(count)]))
    found = jnp.concatenate(found)
    mine = lax.axis_index("subj")
    order = lax.rem(mine - jnp.arange(count, dtype=jnp.int32) + count, count)
    pick = order[:, None] == jnp.arange(count, dtype=jnp.int32)[None, :]
    return jnp.sum(jnp.where(pick, found[None, :], 0), axis=1)


def body(features, token_ticks, offsets, run_lengths, penalty, responses):
    tok_dev, width = features.shape
    group_count = lax.axis_size("subj")
    vox_count = lax.axis_size("vox")
    devices = group_count * vox_count
    slab_width = width // vox_count
    rows_dev = tok_dev * GAP // TICKS
    tr_total = rows_dev * devices
    halo = 3 * TICKS // GAP
    spread = (GAP / TICKS) ** 0.5
    me = lax.axis_index("subj") * vox_count + lax.axis_index("vox")

    before = lax.ppermute(features[-halo:], AXES, [(i, i + 1) for i in range(devices - 1)])
    behind = lax.ppermute(features[:halo], AXES, [(i + 1, i) for i in range(devices - 1)])
    offset_list = all_offsets(offsets)
    far = jnp.full((halo,), -(2**20), jnp.int32)
    padded = jnp.concatenate([far, token_ticks, far])
    near_ticks = lax.dynamic_slice_in_dim(padded, me * tok_dev, tok_dev + 2 * halo, 0)
    tr_rows = me * rows_dev + jnp.arange(rows_dev, dtype=jnp.int32)
    table = jax.vmap(lambda offset: lanczos_rows(near_ticks, offset, tr_rows))(offset_list)
    table = table.reshape(group_count * rows_dev, tok_dev + 2 * halo)

    def term(part, tokens):
        return jnp.dot(part, tokens, preferred_element_type=jnp.float32)

    summed = term(table[:, halo:halo + tok_dev], features)
    summed = summed + term(table[:, :halo], before) + term(table[:, halo + tok_dev:], behind)
    mine = (summed * spread).astype(jnp.bfloat16)
    mine = mine.reshape(group_count, rows_dev, vox_count, slab_width).transpose(0, 2, 1, 3)
    mine = mine.reshape(devices, rows_dev, slab_width)
    interp = lax.all_to_all(mine, AXES, split_axis=0, concat_axis=0, tiled=True)
    interp = interp.reshape(tr_total, slab_width)

    stacked = delay_stack(interp, run_lengths[0], tr_total)
    kernel = gram_sum(stacked, vox_count, width)
    dual_coef = solve(kernel, penalty, responses[0])
    projected = lax.dot_general(
        stacked,
        lax.all_gather(dual_coef, "vox", axis=1, tiled=True),
        (((0,), (0,)), ((), ())),
        preferred_element_type=jnp.float32,
    )
    projected = (projected * (DELAYS * width) ** (-0.5)).astype(jnp.bfloat16)
    return projected.reshape(1, DELAYS, slab_width, projected.shape[1])


def solution(mesh):
    return jax.shard_map(
        body,
        mesh=mesh,
        in_specs=(
            P(("subj", "vox"), None),
            P(),
            P("subj"),
            P("subj", None),
            P("subj"),
            P("subj", None, "vox"),
        ),
        out_specs=P("subj", None, "vox", None),
        check_vma=False,
    )
```

```python
import functools

import jax
import jax.numpy as jnp
from jax import lax
from jax.experimental import pallas as pl
from jax.experimental.pallas import tpu as pltpu
from jax.sharding import PartitionSpec as P

DELAYS = 4
TICKS = 64
GAP = 6
BLOCK = 128
FULL = lax.Precision.HIGHEST
MESH = pl.DeviceIdType.MESH


def delay_stack(interp, lengths, tr_total):
    starts = jnp.cumsum(lengths) - lengths
    tr_steps = jnp.arange(tr_total, dtype=jnp.int32)
    run_first = jnp.max(jnp.where(starts[None, :] <= tr_steps[:, None], starts[None, :], 0), axis=1)
    delayed = []
    for delay_step in range(1, DELAYS + 1):
        moved = jnp.concatenate(
            [jnp.zeros((delay_step, interp.shape[1]), interp.dtype), interp[:-delay_step]], axis=0
        )
        keep_rows = (tr_steps - delay_step >= run_first)[:, None]
        delayed.append(jnp.where(keep_rows, moved, jnp.zeros_like(moved)))
    return jnp.concatenate(delayed, axis=1)


def sinc(x):
    angle = jnp.pi * x
    return jnp.where(x == 0, 1.0, jnp.sin(angle) / jnp.where(x == 0, 1.0, angle))


def spread_kernel(groups, vox, rows_dev, scale, feat_ref, tick_ref, shift_ref, out_ref,
                  edges, shifts, held, send_o, recv_o, send_e, recv_e, send_x, recv_x):
    tok_dev, width = feat_ref.shape
    slab = width // vox
    halo = edges.shape[0] // 2
    devices = groups * vox
    my_group = lax.axis_index("subj")
    my_vox = lax.axis_index("vox")
    me = my_group * vox + my_vox

    def place(device):
        return {"subj": device // vox, "vox": lax.rem(device, vox)}

    barrier = pltpu.get_barrier_semaphore()

    @pl.loop(1, devices)
    def _(turn):
        pl.semaphore_signal(
            barrier, inc=1, device_id=place(lax.rem(me + turn, devices)), device_id_type=MESH
        )

    shifts[my_group] = shift_ref[...]
    pl.semaphore_wait(barrier, devices - 1)

    def tell(turn):
        return pltpu.make_async_remote_copy(
            src_ref=shift_ref, dst_ref=shifts.at[my_group],
            send_sem=send_o.at[turn], recv_sem=recv_o.at[my_group],
            device_id={"subj": lax.rem(my_group + turn, groups)}, device_id_type=MESH,
        )

    def told(turn):
        other = lax.rem(my_group + turn, groups)
        return pltpu.make_async_remote_copy(
            src_ref=shift_ref, dst_ref=shifts.at[other],
            send_sem=send_o.at[turn], recv_sem=recv_o.at[other],
            device_id={"subj": other}, device_id_type=MESH,
        )

    def upward(peer):
        return pltpu.make_async_remote_copy(
            src_ref=feat_ref.at[tok_dev - halo:, :], dst_ref=edges.at[:halo, :],
            send_sem=send_e.at[0], recv_sem=recv_e.at[0],
            device_id=place(peer), device_id_type=MESH,
        )

    def downward(peer):
        return pltpu.make_async_remote_copy(
            src_ref=feat_ref.at[:halo, :], dst_ref=edges.at[halo:, :],
            send_sem=send_e.at[1], recv_sem=recv_e.at[1],
            device_id=place(peer), device_id_type=MESH,
        )

    for turn in range(1, groups):
        tell(turn).start()

    @pl.when(me < devices - 1)
    def _():
        upward(me + 1).start()

    @pl.when(me > 0)
    def _():
        downward(me - 1).start()

    @pl.when(me == 0)
    def _():
        edges[:halo, :] = jnp.zeros((halo, width), edges.dtype)

    @pl.when(me == devices - 1)
    def _():
        edges[halo:, :] = jnp.zeros((halo, width), edges.dtype)

    for turn in range(1, groups):
        told(turn).wait_recv()
    near = tick_ref[0:1, :]
    first = (me * rows_dev + lax.broadcasted_iota(jnp.int32, (16, near.shape[1]), 0)) * TICKS
    pieces = []
    for group in range(groups):
        distance = near - (first + shifts[group][0:1, :])
        inside = jnp.abs(distance) < 3 * TICKS
        scaled = distance.astype(jnp.float32) / TICKS
        shaped = sinc(scaled) * sinc(scaled / 3.0)
        pieces.append(jnp.where(inside, shaped, jnp.zeros_like(shaped)))
    table = jnp.concatenate(pieces, axis=0).astype(jnp.bfloat16)
    inner = table[:, :tok_dev]
    outer = table[:, tok_dev:tok_dev + 2 * halo]

    @pl.when(me > 0)
    def _():
        upward(me - 1).wait_recv()

    @pl.when(me < devices - 1)
    def _():
        downward(me + 1).wait_recv()

    def columns(index):
        return pl.ds(pl.multiple_of(index * slab, slab), slab)

    def rows(index):
        return pl.ds(pl.multiple_of(index * 16, 16), 16)

    def give(group, index):
        return pltpu.make_async_remote_copy(
            src_ref=held.at[rows(group), columns(index)], dst_ref=out_ref.at[rows(me), :],
            send_sem=send_x.at[group * vox + index], recv_sem=recv_x.at[me],
            device_id={"subj": group, "vox": index}, device_id_type=MESH,
        )

    def taken(source):
        return pltpu.make_async_remote_copy(
            src_ref=held.at[rows(0), columns(0)], dst_ref=out_ref.at[rows(source), :],
            send_sem=send_x.at[source], recv_sem=recv_x.at[source],
            device_id=place(source), device_id_type=MESH,
        )

    def make(index):
        summed = jnp.dot(inner, feat_ref[:, columns(index)], preferred_element_type=jnp.float32)
        summed = summed + jnp.dot(
            outer, edges[:, columns(index)], preferred_element_type=jnp.float32
        )
        held[:, columns(index)] = (summed * scale).astype(jnp.bfloat16)

    @pl.loop(1, vox)
    def _(step):
        index = lax.rem(my_vox + step, vox)
        make(index)
        for turn in range(groups):
            give(lax.rem(my_group + turn, groups), index).start()

    make(my_vox)
    for turn in range(1, groups):
        give(lax.rem(my_group + turn, groups), my_vox).start()
    out_ref[rows(me), :] = held[rows(my_group), columns(my_vox)]

    @pl.loop(1, devices)
    def _(turn):
        other = lax.rem(me + turn, devices)
        taken(other).wait_recv()

    @pl.loop(1, devices)
    def _(turn):
        other = lax.rem(me + turn, devices)
        give(other // vox, lax.rem(other, vox)).wait_send()

    for turn in range(1, groups):
        tell(turn).wait_send()

    @pl.when(me < devices - 1)
    def _():
        upward(me + 1).wait_send()

    @pl.when(me > 0)
    def _():
        downward(me - 1).wait_send()


def spread_interp(features, ticks, shift, groups, vox, rows_dev, halo):
    tok_dev, width = features.shape
    devices = groups * vox
    slab = width // vox
    lanes = ticks.shape[1]
    return pl.pallas_call(
        functools.partial(spread_kernel, groups, vox, rows_dev, (GAP / TICKS) ** 0.5),
        out_shape=jax.ShapeDtypeStruct((devices * 16, slab), jnp.bfloat16),
        in_specs=[pl.BlockSpec(memory_space=pltpu.VMEM)] * 3,
        out_specs=pl.BlockSpec(memory_space=pltpu.VMEM),
        scratch_shapes=[
            pltpu.VMEM((2 * halo, width), jnp.bfloat16),
            pltpu.VMEM((groups, 8, lanes), jnp.int32),
            pltpu.VMEM((groups * 16, width), jnp.bfloat16),
            pltpu.SemaphoreType.DMA((groups,)),
            pltpu.SemaphoreType.DMA((groups,)),
            pltpu.SemaphoreType.DMA((2,)),
            pltpu.SemaphoreType.DMA((2,)),
            pltpu.SemaphoreType.DMA((devices,)),
            pltpu.SemaphoreType.DMA((devices,)),
        ],
        compiler_params=pltpu.CompilerParams(
            collective_id=1, has_side_effects=True, vmem_limit_bytes=32 * 2**20
        ),
        name="spread_interp",
    )(features, ticks, shift)


def gram_kernel(n, scale, stacked_ref, out_ref, part, land, send_a, recv_a, send_b, recv_b):
    me = lax.axis_index("vox")
    total = out_ref.shape[0]
    rows = total // n
    barrier = pltpu.get_barrier_semaphore()
    for step in range(1, n):
        pl.semaphore_signal(
            barrier, inc=1, device_id={"vox": lax.rem(me + step, n)}, device_id_type=MESH
        )

    @pl.loop(0, total // BLOCK)
    def _(block):
        here = pl.ds(pl.multiple_of(block * BLOCK, BLOCK), BLOCK)
        part[here, :] = lax.dot_general(
            stacked_ref[here, :], stacked_ref[...], (((1,), (1,)), ((), ())),
            preferred_element_type=jnp.float32,
        )

    pl.semaphore_wait(barrier, n - 1)

    def rows_of(owner):
        return pl.ds(pl.multiple_of(owner * rows, rows), rows)

    def share(step):
        peer = lax.rem(me + step, n)
        return pltpu.make_async_remote_copy(
            src_ref=part.at[rows_of(peer), :], dst_ref=land.at[me],
            send_sem=send_a.at[step], recv_sem=recv_a.at[me],
            device_id={"vox": peer}, device_id_type=MESH,
        )

    def arrived(step):
        peer = lax.rem(me + step, n)
        return pltpu.make_async_remote_copy(
            src_ref=part.at[rows_of(me), :], dst_ref=land.at[peer],
            send_sem=send_a.at[step], recv_sem=recv_a.at[peer],
            device_id={"vox": peer}, device_id_type=MESH,
        )

    def spread(step):
        peer = lax.rem(me + step, n)
        return pltpu.make_async_remote_copy(
            src_ref=out_ref.at[rows_of(me), :], dst_ref=out_ref.at[rows_of(me), :],
            send_sem=send_b.at[step], recv_sem=recv_b.at[me],
            device_id={"vox": peer}, device_id_type=MESH,
        )

    def spread_in(step):
        peer = lax.rem(me + step, n)
        return pltpu.make_async_remote_copy(
            src_ref=out_ref.at[rows_of(peer), :], dst_ref=out_ref.at[rows_of(peer), :],
            send_sem=send_b.at[step], recv_sem=recv_b.at[peer],
            device_id={"vox": peer}, device_id_type=MESH,
        )

    for step in range(1, n):
        share(step).start()
    total_rows = part[rows_of(me), :]
    for step in range(1, n):
        arrived(step).wait_recv()
        total_rows = total_rows + land[lax.rem(me + step, n)]
    out_ref[rows_of(me), :] = total_rows * scale
    for step in range(1, n):
        spread(step).start()
    for step in range(1, n):
        spread_in(step).wait_recv()
    for step in range(1, n):
        share(step).wait_send()
        spread(step).wait_send()


def gram_sum(stacked, n, width):
    total = stacked.shape[0]
    rows = total // n
    return pl.pallas_call(
        functools.partial(gram_kernel, n, 1.0 / (DELAYS * width)),
        out_shape=jax.ShapeDtypeStruct((total, total), jnp.float32),
        in_specs=[pl.BlockSpec(memory_space=pltpu.VMEM)],
        out_specs=pl.BlockSpec(memory_space=pltpu.VMEM),
        scratch_shapes=[
            pltpu.VMEM((total, total), jnp.float32),
            pltpu.VMEM((n, rows, total), jnp.float32),
            pltpu.SemaphoreType.DMA((n,)),
            pltpu.SemaphoreType.DMA((n,)),
            pltpu.SemaphoreType.DMA((n,)),
            pltpu.SemaphoreType.DMA((n,)),
        ],
        compiler_params=pltpu.CompilerParams(
            collective_id=0, has_side_effects=True, vmem_limit_bytes=48 * 2**20
        ),
        name="gram_sum",
    )(stacked)


def full_dot(a, b):
    return jnp.dot(a, b, precision=FULL, preferred_element_type=jnp.float32)


def solve_kernel(kernel_ref, penalty_ref, targets_ref, out_ref, work, pair):
    total, voxels = targets_ref.shape
    blocks = total // BLOCK
    penalty = penalty_ref[0]
    row = lax.broadcasted_iota(jnp.int32, (BLOCK, BLOCK), 0)
    col = lax.broadcasted_iota(jnp.int32, (BLOCK, BLOCK), 1)
    eye = jnp.where(row == col, 1.0, 0.0).astype(jnp.float32)
    work[:, :total] = kernel_ref[...]
    work[:, total:] = targets_ref[...]
    for k in range(blocks):
        here = slice(k * BLOCK, (k + 1) * BLOCK)
        work[here, here] = work[here, here] + penalty * eye
    low = penalty * 0.9
    for k in range(blocks):
        here = slice(k * BLOCK, (k + 1) * BLOCK)
        after = (k + 1) * BLOCK
        diagonal = work[here, here]
        high = jnp.max(jnp.sum(jnp.abs(diagonal), axis=1))
        first = 2.0 / (low + high)
        pair[:BLOCK] = first * eye
        pair[BLOCK:] = first * diagonal

        def going(least):
            return least < 1.0 - 2.0**-12

        def step(least):
            inner = least * (2.0 - least)
            grow = 2.0 / (1.0 + inner)
            pair[...] = full_dot(pair[...], grow * (2.0 * eye - pair[BLOCK:]))
            return inner * grow

        lax.while_loop(going, step, low * first)
        inverse = pair[:BLOCK]
        inverse = inverse + full_dot(inverse, eye - full_dot(diagonal, inverse))
        ahead = full_dot(inverse, work[here, after:])
        work[here, after:] = ahead
        rest = blocks - 1 - k
        if 0 < rest <= 2:
            work[after:total, after:] -= full_dot(work[after:total, here], ahead)
        elif rest:

            @pl.loop(k + 1, blocks)
            def _(below):
                there = pl.ds(pl.multiple_of(below * BLOCK, BLOCK), BLOCK)
                work[there, after:] -= full_dot(work[there, here], work[here, after:])

    for k in range(blocks - 2, -1, -1):
        here = slice(k * BLOCK, (k + 1) * BLOCK)
        after = (k + 1) * BLOCK
        work[here, total:] -= full_dot(work[here, after:total], work[after:total, total:])
    out_ref[...] = work[:, total:].astype(out_ref.dtype)


def solve(kernel, penalty, targets):
    total, voxels = targets.shape
    return pl.pallas_call(
        solve_kernel,
        out_shape=jax.ShapeDtypeStruct((total, voxels), jnp.bfloat16),
        in_specs=[
            pl.BlockSpec(memory_space=pltpu.VMEM),
            pl.BlockSpec(memory_space=pltpu.SMEM),
            pl.BlockSpec(memory_space=pltpu.VMEM),
        ],
        out_specs=pl.BlockSpec(memory_space=pltpu.VMEM),
        scratch_shapes=[
            pltpu.VMEM((total, total + voxels), jnp.float32),
            pltpu.VMEM((2 * BLOCK, BLOCK), jnp.float32),
        ],
        compiler_params=pltpu.CompilerParams(vmem_limit_bytes=48 * 2**20),
        name="ridge_solve",
    )(kernel, penalty, targets)


def body(features, token_ticks, offsets, run_lengths, penalty, responses):
    tok_dev, width = features.shape
    group_count = lax.axis_size("subj")
    vox_count = lax.axis_size("vox")
    devices = group_count * vox_count
    slab_width = width // vox_count
    rows_dev = tok_dev * GAP // TICKS
    tr_total = rows_dev * devices
    halo = 3 * TICKS // GAP
    me = lax.axis_index("subj") * vox_count + lax.axis_index("vox")

    far = jnp.full((tok_dev,), -(2**20), jnp.int32)
    padded = jnp.concatenate([far, token_ticks, far])
    near = lax.dynamic_slice_in_dim(padded, me * tok_dev + tok_dev - halo, tok_dev + 2 * halo, 0)
    ticks = jnp.concatenate(
        [near[halo:halo + tok_dev], near[:halo], near[halo + tok_dev:], far[:tok_dev - 2 * halo]]
    )
    ticks = jnp.broadcast_to(ticks, (8, 2 * tok_dev))
    shift = jnp.broadcast_to(offsets[0], (8, 2 * tok_dev))
    blocks = spread_interp(features, ticks, shift, group_count, vox_count, rows_dev, halo)
    interp = blocks.reshape(devices, 16, slab_width)[:, :rows_dev].reshape(tr_total, slab_width)

    stacked = delay_stack(interp, run_lengths[0], tr_total)
    kernel = gram_sum(stacked, vox_count, width)
    dual_coef = solve(kernel, penalty, responses[0])
    projected = lax.dot_general(
        stacked,
        lax.all_gather(dual_coef, "vox", axis=1, tiled=True),
        (((0,), (0,)), ((), ())),
        preferred_element_type=jnp.float32,
    )
    projected = (projected * (DELAYS * width) ** (-0.5)).astype(jnp.bfloat16)
    return projected.reshape(1, DELAYS, slab_width, projected.shape[1])


def solution(mesh):
    return jax.shard_map(
        body,
        mesh=mesh,
        in_specs=(
            P(("subj", "vox"), None),
            P(),
            P("subj"),
            P("subj", None),
            P("subj"),
            P("subj", None, "vox"),
        ),
        out_specs=P("subj", None, "vox", None),
        check_vma=False,
    )
```

```python
import functools

import jax
import jax.numpy as jnp
from jax import lax
from jax.experimental import pallas as pl
from jax.experimental.pallas import tpu as pltpu
from jax.sharding import PartitionSpec as P

DELAYS = 4
TICKS = 64
GAP = 6
BLOCK = 128
FULL = lax.Precision.HIGHEST
MESH = pl.DeviceIdType.MESH


def delay_stack(interp, lengths, tr_total):
    runs = jnp.arange(lengths.shape[0])
    starts = jnp.sum(jnp.where(runs[None, :] < runs[:, None], lengths[None, :], 0), axis=1)
    tr_steps = jnp.arange(tr_total, dtype=jnp.int32)
    run_first = jnp.max(jnp.where(starts[None, :] <= tr_steps[:, None], starts[None, :], 0), axis=1)
    delayed = []
    for delay_step in range(1, DELAYS + 1):
        moved = jnp.concatenate(
            [jnp.zeros((delay_step, interp.shape[1]), interp.dtype), interp[:-delay_step]], axis=0
        )
        keep_rows = (tr_steps - delay_step >= run_first)[:, None]
        delayed.append(jnp.where(keep_rows, moved, jnp.zeros_like(moved)))
    return jnp.concatenate(delayed, axis=1)


def sinc(x):
    angle = jnp.pi * x
    return jnp.where(x == 0, 1.0, jnp.sin(angle) / jnp.where(x == 0, 1.0, angle))


def spread_kernel(groups, vox, rows_dev, scale, feat_ref, tick_ref, shift_ref, out_ref,
                  edges, shifts, held, send_o, recv_o, send_e, recv_e, send_x, recv_x):
    tok_dev, width = feat_ref.shape
    slab = width // vox
    halo = edges.shape[0] // 2
    devices = groups * vox
    my_group = lax.axis_index("subj")
    my_vox = lax.axis_index("vox")
    me = my_group * vox + my_vox

    def place(device):
        return {"subj": device // vox, "vox": lax.rem(device, vox)}

    barrier = pltpu.get_barrier_semaphore()

    @pl.loop(1, devices)
    def _(turn):
        pl.semaphore_signal(
            barrier, inc=1, device_id=place(lax.rem(me + turn, devices)), device_id_type=MESH
        )

    shifts[my_group] = shift_ref[...]
    pl.semaphore_wait(barrier, devices - 1)

    def tell(turn):
        return pltpu.make_async_remote_copy(
            src_ref=shift_ref, dst_ref=shifts.at[my_group],
            send_sem=send_o.at[turn], recv_sem=recv_o.at[my_group],
            device_id={"subj": lax.rem(my_group + turn, groups)}, device_id_type=MESH,
        )

    def told(turn):
        other = lax.rem(my_group + turn, groups)
        return pltpu.make_async_remote_copy(
            src_ref=shift_ref, dst_ref=shifts.at[other],
            send_sem=send_o.at[turn], recv_sem=recv_o.at[other],
            device_id={"subj": other}, device_id_type=MESH,
        )

    def upward(peer):
        return pltpu.make_async_remote_copy(
            src_ref=feat_ref.at[tok_dev - halo:, :], dst_ref=edges.at[:halo, :],
            send_sem=send_e.at[0], recv_sem=recv_e.at[0],
            device_id=place(peer), device_id_type=MESH,
        )

    def downward(peer):
        return pltpu.make_async_remote_copy(
            src_ref=feat_ref.at[:halo, :], dst_ref=edges.at[halo:, :],
            send_sem=send_e.at[1], recv_sem=recv_e.at[1],
            device_id=place(peer), device_id_type=MESH,
        )

    for turn in range(1, groups):
        tell(turn).start()

    @pl.when(me < devices - 1)
    def _():
        upward(me + 1).start()

    @pl.when(me > 0)
    def _():
        downward(me - 1).start()

    @pl.when(me == 0)
    def _():
        edges[:halo, :] = jnp.zeros((halo, width), edges.dtype)

    @pl.when(me == devices - 1)
    def _():
        edges[halo:, :] = jnp.zeros((halo, width), edges.dtype)

    for turn in range(1, groups):
        told(turn).wait_recv()
    near = tick_ref[0:1, :]
    first = (me * rows_dev + lax.broadcasted_iota(jnp.int32, (16, near.shape[1]), 0)) * TICKS
    pieces = []
    for group in range(groups):
        distance = near - (first + shifts[group][0:1, :])
        inside = jnp.abs(distance) < 3 * TICKS
        scaled = distance.astype(jnp.float32) / TICKS
        shaped = sinc(scaled) * sinc(scaled / 3.0)
        pieces.append(jnp.where(inside, shaped, jnp.zeros_like(shaped)))
    table = jnp.concatenate(pieces, axis=0).astype(jnp.bfloat16)
    inner = table[:, :tok_dev]
    outer = table[:, tok_dev:tok_dev + 2 * halo]

    @pl.when(me > 0)
    def _():
        upward(me - 1).wait_recv()

    @pl.when(me < devices - 1)
    def _():
        downward(me + 1).wait_recv()

    def columns(index):
        return pl.ds(pl.multiple_of(index * slab, slab), slab)

    def rows(index):
        return pl.ds(pl.multiple_of(index * 16, 16), 16)

    def give(group, index):
        return pltpu.make_async_remote_copy(
            src_ref=held.at[rows(group), columns(index)], dst_ref=out_ref.at[rows(me), :],
            send_sem=send_x.at[group * vox + index], recv_sem=recv_x.at[me],
            device_id={"subj": group, "vox": index}, device_id_type=MESH,
        )

    def taken(source):
        return pltpu.make_async_remote_copy(
            src_ref=held.at[rows(0), columns(0)], dst_ref=out_ref.at[rows(source), :],
            send_sem=send_x.at[source], recv_sem=recv_x.at[source],
            device_id=place(source), device_id_type=MESH,
        )

    def make(index):
        summed = jnp.dot(inner, feat_ref[:, columns(index)], preferred_element_type=jnp.float32)
        summed = summed + jnp.dot(
            outer, edges[:, columns(index)], preferred_element_type=jnp.float32
        )
        held[:, columns(index)] = (summed * scale).astype(jnp.bfloat16)

    @pl.loop(1, vox)
    def _(step):
        index = lax.rem(my_vox + step, vox)
        make(index)
        for turn in range(groups):
            give(lax.rem(my_group + turn, groups), index).start()

    make(my_vox)
    for turn in range(1, groups):
        give(lax.rem(my_group + turn, groups), my_vox).start()
    out_ref[rows(me), :] = held[rows(my_group), columns(my_vox)]

    @pl.loop(1, devices)
    def _(turn):
        other = lax.rem(me + turn, devices)
        taken(other).wait_recv()

    @pl.loop(1, devices)
    def _(turn):
        other = lax.rem(me + turn, devices)
        give(other // vox, lax.rem(other, vox)).wait_send()

    for turn in range(1, groups):
        tell(turn).wait_send()

    @pl.when(me < devices - 1)
    def _():
        upward(me + 1).wait_send()

    @pl.when(me > 0)
    def _():
        downward(me - 1).wait_send()


def spread_interp(features, ticks, shift, groups, vox, rows_dev, halo):
    tok_dev, width = features.shape
    devices = groups * vox
    slab = width // vox
    lanes = ticks.shape[1]
    return pl.pallas_call(
        functools.partial(spread_kernel, groups, vox, rows_dev, (GAP / TICKS) ** 0.5),
        out_shape=jax.ShapeDtypeStruct((devices * 16, slab), jnp.bfloat16),
        in_specs=[pl.BlockSpec(memory_space=pltpu.VMEM)] * 3,
        out_specs=pl.BlockSpec(memory_space=pltpu.VMEM),
        scratch_shapes=[
            pltpu.VMEM((2 * halo, width), jnp.bfloat16),
            pltpu.VMEM((groups, 8, lanes), jnp.int32),
            pltpu.VMEM((groups * 16, width), jnp.bfloat16),
            pltpu.SemaphoreType.DMA((groups,)),
            pltpu.SemaphoreType.DMA((groups,)),
            pltpu.SemaphoreType.DMA((2,)),
            pltpu.SemaphoreType.DMA((2,)),
            pltpu.SemaphoreType.DMA((devices,)),
            pltpu.SemaphoreType.DMA((devices,)),
        ],
        compiler_params=pltpu.CompilerParams(
            collective_id=1, has_side_effects=True, vmem_limit_bytes=32 * 2**20
        ),
        name="spread_interp",
    )(features, ticks, shift)


def gram_kernel(n, scale, stacked_ref, out_ref, part, land, send_a, recv_a, send_b, recv_b):
    me = lax.axis_index("vox")
    total = out_ref.shape[0]
    rows = total // n
    barrier = pltpu.get_barrier_semaphore()
    for step in range(1, n):
        pl.semaphore_signal(
            barrier, inc=1, device_id={"vox": lax.rem(me + step, n)}, device_id_type=MESH
        )

    @pl.loop(0, total // BLOCK)
    def _(block):
        here = pl.ds(pl.multiple_of(block * BLOCK, BLOCK), BLOCK)
        part[here, :] = lax.dot_general(
            stacked_ref[here, :], stacked_ref[...], (((1,), (1,)), ((), ())),
            preferred_element_type=jnp.float32,
        )

    pl.semaphore_wait(barrier, n - 1)

    def rows_of(owner):
        return pl.ds(pl.multiple_of(owner * rows, rows), rows)

    def share(step):
        peer = lax.rem(me + step, n)
        return pltpu.make_async_remote_copy(
            src_ref=part.at[rows_of(peer), :], dst_ref=land.at[me],
            send_sem=send_a.at[step], recv_sem=recv_a.at[me],
            device_id={"vox": peer}, device_id_type=MESH,
        )

    def arrived(step):
        peer = lax.rem(me + step, n)
        return pltpu.make_async_remote_copy(
            src_ref=part.at[rows_of(me), :], dst_ref=land.at[peer],
            send_sem=send_a.at[step], recv_sem=recv_a.at[peer],
            device_id={"vox": peer}, device_id_type=MESH,
        )

    def spread(step):
        peer = lax.rem(me + step, n)
        return pltpu.make_async_remote_copy(
            src_ref=out_ref.at[rows_of(me), :], dst_ref=out_ref.at[rows_of(me), :],
            send_sem=send_b.at[step], recv_sem=recv_b.at[me],
            device_id={"vox": peer}, device_id_type=MESH,
        )

    def spread_in(step):
        peer = lax.rem(me + step, n)
        return pltpu.make_async_remote_copy(
            src_ref=out_ref.at[rows_of(peer), :], dst_ref=out_ref.at[rows_of(peer), :],
            send_sem=send_b.at[step], recv_sem=recv_b.at[peer],
            device_id={"vox": peer}, device_id_type=MESH,
        )

    for step in range(1, n):
        share(step).start()
    total_rows = part[rows_of(me), :]
    for step in range(1, n):
        arrived(step).wait_recv()
        total_rows = total_rows + land[lax.rem(me + step, n)]
    out_ref[rows_of(me), :] = total_rows * scale
    for step in range(1, n):
        spread(step).start()
    for step in range(1, n):
        spread_in(step).wait_recv()
    for step in range(1, n):
        share(step).wait_send()
        spread(step).wait_send()


def gram_sum(stacked, n, width):
    total = stacked.shape[0]
    rows = total // n
    return pl.pallas_call(
        functools.partial(gram_kernel, n, 1.0 / (DELAYS * width)),
        out_shape=jax.ShapeDtypeStruct((total, total), jnp.float32),
        in_specs=[pl.BlockSpec(memory_space=pltpu.VMEM)],
        out_specs=pl.BlockSpec(memory_space=pltpu.VMEM),
        scratch_shapes=[
            pltpu.VMEM((total, total), jnp.float32),
            pltpu.VMEM((n, rows, total), jnp.float32),
            pltpu.SemaphoreType.DMA((n,)),
            pltpu.SemaphoreType.DMA((n,)),
            pltpu.SemaphoreType.DMA((n,)),
            pltpu.SemaphoreType.DMA((n,)),
        ],
        compiler_params=pltpu.CompilerParams(
            collective_id=0, has_side_effects=True, vmem_limit_bytes=48 * 2**20
        ),
        name="gram_sum",
    )(stacked)


def full_dot(a, b):
    return jnp.dot(a, b, precision=FULL, preferred_element_type=jnp.float32)


def ridge(work, pair, total, penalty):
    blocks = total // BLOCK
    row = lax.broadcasted_iota(jnp.int32, (BLOCK, BLOCK), 0)
    col = lax.broadcasted_iota(jnp.int32, (BLOCK, BLOCK), 1)
    eye = jnp.where(row == col, 1.0, 0.0).astype(jnp.float32)
    for k in range(blocks):
        here = slice(k * BLOCK, (k + 1) * BLOCK)
        work[here, here] = work[here, here] + penalty * eye
    low = penalty * 0.9
    for k in range(blocks):
        here = slice(k * BLOCK, (k + 1) * BLOCK)
        after = (k + 1) * BLOCK
        diagonal = work[here, here]
        high = jnp.max(jnp.sum(jnp.abs(diagonal), axis=1))
        first = 2.0 / (low + high)
        pair[:BLOCK] = first * eye
        pair[BLOCK:] = first * diagonal

        def going(least):
            return least < 1.0 - 2.0**-12

        def step(least):
            inner = least * (2.0 - least)
            grow = 2.0 / (1.0 + inner)
            pair[...] = full_dot(pair[...], grow * (2.0 * eye - pair[BLOCK:]))
            return inner * grow

        lax.while_loop(going, step, low * first)
        inverse = pair[:BLOCK]
        inverse = inverse + full_dot(inverse, eye - full_dot(diagonal, inverse))
        ahead = full_dot(inverse, work[here, after:])
        work[here, after:] = ahead
        rest = blocks - 1 - k
        if 0 < rest <= 2:
            work[after:total, after:] -= full_dot(work[after:total, here], ahead)
        elif rest:

            @pl.loop(k + 1, blocks)
            def _(below):
                there = pl.ds(pl.multiple_of(below * BLOCK, BLOCK), BLOCK)
                work[there, after:] -= full_dot(work[there, here], work[here, after:])

    for k in range(blocks - 2, -1, -1):
        here = slice(k * BLOCK, (k + 1) * BLOCK)
        after = (k + 1) * BLOCK
        if blocks - 1 - k <= 2:
            work[here, total:] -= full_dot(work[here, after:total], work[after:total, total:])
        else:
            for below in range(k + 1, blocks):
                there = slice(below * BLOCK, (below + 1) * BLOCK)
                work[here, total:] -= full_dot(work[here, there], work[there, total:])


def fetch_all(kernel_ref, targets_ref, work, fetched):
    parts, total, voxels = targets_ref.shape
    fetches = [pltpu.make_async_copy(kernel_ref, work.at[:, :total], fetched.at[parts])]
    for part in range(parts):
        columns = slice(total + part * voxels, total + (part + 1) * voxels)
        fetches.append(
            pltpu.make_async_copy(targets_ref.at[part], work.at[:, columns], fetched.at[part])
        )
    for fetch in fetches:
        fetch.start()
    for fetch in fetches:
        fetch.wait()


def dual_kernel(kernel_ref, penalty_ref, targets_ref, out_ref, work, pair, fetched):
    total = targets_ref.shape[1]
    fetch_all(kernel_ref, targets_ref, work, fetched)
    ridge(work, pair, total, penalty_ref[0])
    out_ref[...] = work[:, total:].astype(out_ref.dtype)


def solve_kernel(scale, kernel_ref, penalty_ref, targets_ref, stacked_ref, out_ref,
                 work, pair, dual, result, done, fetched):
    total = targets_ref.shape[1]
    fetch_all(kernel_ref, targets_ref, work, fetched)
    ridge(work, pair, total, penalty_ref[0])
    dual[...] = work[:, total:].astype(dual.dtype)
    slab = result.shape[1]

    def leave(step):
        return pltpu.make_async_copy(result.at[step], out_ref.at[0, step], done.at[step])

    for step in range(DELAYS):
        projected = lax.dot_general(
            stacked_ref[:, step * slab:(step + 1) * slab], dual[...], (((0,), (0,)), ((), ())),
            preferred_element_type=jnp.float32,
        )
        result[step] = (projected * scale).astype(result.dtype)
        leave(step).start()
    for step in range(DELAYS):
        leave(step).wait()


def solve_dual(kernel, penalty, targets):
    total, voxels = targets.shape
    away = pl.BlockSpec(memory_space=pl.ANY)
    return pl.pallas_call(
        dual_kernel,
        out_shape=jax.ShapeDtypeStruct((total, voxels), jnp.bfloat16),
        in_specs=[away, pl.BlockSpec(memory_space=pltpu.SMEM), away],
        out_specs=pl.BlockSpec(memory_space=pltpu.VMEM),
        scratch_shapes=[
            pltpu.VMEM((total, total + voxels), jnp.float32),
            pltpu.VMEM((2 * BLOCK, BLOCK), jnp.float32),
            pltpu.SemaphoreType.DMA((2,)),
        ],
        compiler_params=pltpu.CompilerParams(vmem_limit_bytes=48 * 2**20),
        name="ridge_dual",
    )(kernel, penalty, targets[None])


def solve(kernel, penalty, targets, stacked, width):
    parts, total, voxels = targets.shape
    slab = stacked.shape[1] // DELAYS
    block = pl.BlockSpec(memory_space=pltpu.VMEM)
    away = pl.BlockSpec(memory_space=pl.ANY)
    return pl.pallas_call(
        functools.partial(solve_kernel, (DELAYS * width) ** (-0.5)),
        out_shape=jax.ShapeDtypeStruct((1, DELAYS, slab, parts * voxels), jnp.bfloat16),
        in_specs=[away, pl.BlockSpec(memory_space=pltpu.SMEM), away, block],
        out_specs=pl.BlockSpec(memory_space=pl.ANY),
        scratch_shapes=[
            pltpu.VMEM((total, total + parts * voxels), jnp.float32),
            pltpu.VMEM((2 * BLOCK, BLOCK), jnp.float32),
            pltpu.VMEM((total, parts * voxels), jnp.bfloat16),
            pltpu.VMEM((DELAYS, slab, parts * voxels), jnp.bfloat16),
            pltpu.SemaphoreType.DMA((DELAYS,)),
            pltpu.SemaphoreType.DMA((parts + 1,)),
        ],
        compiler_params=pltpu.CompilerParams(vmem_limit_bytes=60 * 2**20),
        name="ridge_solve",
    )(kernel, penalty, targets, stacked)


def body(features, token_ticks, offsets, run_lengths, penalty, responses):
    tok_dev, width = features.shape
    group_count = lax.axis_size("subj")
    vox_count = lax.axis_size("vox")
    devices = group_count * vox_count
    slab_width = width // vox_count
    rows_dev = tok_dev * GAP // TICKS
    tr_total = rows_dev * devices
    halo = 3 * TICKS // GAP
    me = lax.axis_index("subj") * vox_count + lax.axis_index("vox")
    whole = tr_total <= 4 * BLOCK
    if whole:
        targets = lax.all_gather(responses[0], "vox", axis=0)

    far = jnp.full((tok_dev,), -(2**20), jnp.int32)
    padded = jnp.concatenate([far, token_ticks, far])
    near = lax.dynamic_slice_in_dim(padded, me * tok_dev + tok_dev - halo, tok_dev + 2 * halo, 0)
    ticks = jnp.concatenate(
        [near[halo:halo + tok_dev], near[:halo], near[halo + tok_dev:], far[:tok_dev - 2 * halo]]
    )
    ticks = jnp.broadcast_to(ticks, (8, 2 * tok_dev))
    shift = jnp.broadcast_to(offsets[0], (8, 2 * tok_dev))
    blocks = spread_interp(features, ticks, shift, group_count, vox_count, rows_dev, halo)
    interp = blocks.reshape(devices, 16, slab_width)[:, :rows_dev].reshape(tr_total, slab_width)

    stacked = delay_stack(interp, run_lengths[0], tr_total)
    kernel = gram_sum(stacked, vox_count, width)
    if whole:
        return solve(kernel, penalty, targets, stacked, width)
    dual_coef = solve_dual(kernel, penalty, responses[0])
    projected = lax.dot_general(
        stacked,
        lax.all_gather(dual_coef, "vox", axis=1, tiled=True),
        (((0,), (0,)), ((), ())),
        preferred_element_type=jnp.float32,
    )
    projected = (projected * (DELAYS * width) ** (-0.5)).astype(jnp.bfloat16)
    return projected.reshape(1, DELAYS, slab_width, projected.shape[1])


def solution(mesh):
    return jax.shard_map(
        body,
        mesh=mesh,
        in_specs=(
            P(("subj", "vox"), None),
            P(),
            P("subj"),
            P("subj", None),
            P("subj"),
            P("subj", None, "vox"),
        ),
        out_specs=P("subj", None, "vox", None),
        check_vma=False,
    )
```

```python
import functools

import jax
import jax.numpy as jnp
from jax import lax
from jax.experimental import pallas as pl
from jax.experimental.pallas import tpu as pltpu
from jax.sharding import PartitionSpec as P

DELAYS = 4
TICKS = 64
GAP = 6
BLOCK = 128
FULL = lax.Precision.HIGHEST
MESH = pl.DeviceIdType.MESH


def delay_stack(interp, lengths, tr_total):
    runs = jnp.arange(lengths.shape[0])
    starts = jnp.sum(jnp.where(runs[None, :] < runs[:, None], lengths[None, :], 0), axis=1)
    tr_steps = jnp.arange(tr_total, dtype=jnp.int32)
    run_first = jnp.max(jnp.where(starts[None, :] <= tr_steps[:, None], starts[None, :], 0), axis=1)
    delayed = []
    for delay_step in range(1, DELAYS + 1):
        moved = jnp.concatenate(
            [jnp.zeros((delay_step, interp.shape[1]), interp.dtype), interp[:-delay_step]], axis=0
        )
        keep_rows = (tr_steps - delay_step >= run_first)[:, None]
        delayed.append(jnp.where(keep_rows, moved, jnp.zeros_like(moved)))
    return jnp.concatenate(delayed, axis=1)


def sinc(x):
    angle = jnp.pi * x
    return jnp.where(x == 0, 1.0, jnp.sin(angle) / jnp.where(x == 0, 1.0, angle))


def spread_kernel(groups, vox, rows_dev, scale, share, feat_ref, tick_ref, shift_ref, target_ref,
                  out_ref, half_ref, edges, shifts, held, send_o, recv_o, send_e, recv_e,
                  send_x, recv_x, send_r, recv_r):
    tok_dev, width = feat_ref.shape
    slab = width // vox
    halo = edges.shape[0] // 2
    devices = groups * vox
    my_group = lax.axis_index("subj")
    my_vox = lax.axis_index("vox")
    me = my_group * vox + my_vox

    def place(device):
        return {"subj": device // vox, "vox": lax.rem(device, vox)}

    barrier = pltpu.get_barrier_semaphore()

    @pl.loop(1, devices)
    def _(turn):
        pl.semaphore_signal(
            barrier, inc=1, device_id=place(lax.rem(me + turn, devices)), device_id_type=MESH
        )

    shifts[my_group] = shift_ref[...]
    pl.semaphore_wait(barrier, devices - 1)

    def tell(turn):
        return pltpu.make_async_remote_copy(
            src_ref=shift_ref, dst_ref=shifts.at[my_group],
            send_sem=send_o.at[turn], recv_sem=recv_o.at[my_group],
            device_id={"subj": lax.rem(my_group + turn, groups)}, device_id_type=MESH,
        )

    def told(turn):
        other = lax.rem(my_group + turn, groups)
        return pltpu.make_async_remote_copy(
            src_ref=shift_ref, dst_ref=shifts.at[other],
            send_sem=send_o.at[turn], recv_sem=recv_o.at[other],
            device_id={"subj": other}, device_id_type=MESH,
        )

    def upward(peer):
        return pltpu.make_async_remote_copy(
            src_ref=feat_ref.at[tok_dev - halo:, :], dst_ref=edges.at[:halo, :],
            send_sem=send_e.at[0], recv_sem=recv_e.at[0],
            device_id=place(peer), device_id_type=MESH,
        )

    def downward(peer):
        return pltpu.make_async_remote_copy(
            src_ref=feat_ref.at[:halo, :], dst_ref=edges.at[halo:, :],
            send_sem=send_e.at[1], recv_sem=recv_e.at[1],
            device_id=place(peer), device_id_type=MESH,
        )

    chips = vox // 2
    chip, core = my_vox // 2, lax.rem(my_vox, 2)

    def lend(turn):
        other = lax.rem(chip + turn, chips)
        return pltpu.make_async_remote_copy(
            src_ref=target_ref, dst_ref=half_ref.at[chip],
            send_sem=send_r.at[turn], recv_sem=recv_r.at[chip],
            device_id={"vox": other * 2 + core}, device_id_type=MESH,
        )

    def lent(turn):
        other = lax.rem(chip + turn, chips)
        return pltpu.make_async_remote_copy(
            src_ref=target_ref, dst_ref=half_ref.at[other],
            send_sem=send_r.at[turn], recv_sem=recv_r.at[other],
            device_id={"vox": other * 2 + core}, device_id_type=MESH,
        )

    for turn in range(1, groups):
        tell(turn).start()

    @pl.when(me < devices - 1)
    def _():
        upward(me + 1).start()

    @pl.when(me > 0)
    def _():
        downward(me - 1).start()

    @pl.when(me == 0)
    def _():
        edges[:halo, :] = jnp.zeros((halo, width), edges.dtype)

    @pl.when(me == devices - 1)
    def _():
        edges[halo:, :] = jnp.zeros((halo, width), edges.dtype)

    if share:
        for turn in range(1, chips):
            lend(turn).start()
        half_ref[chip] = target_ref[...]

    for turn in range(1, groups):
        told(turn).wait_recv()
    near = tick_ref[0:1, :]
    first = (me * rows_dev + lax.broadcasted_iota(jnp.int32, (16, near.shape[1]), 0)) * TICKS
    pieces = []
    for group in range(groups):
        distance = near - (first + shifts[group][0:1, :])
        inside = jnp.abs(distance) < 3 * TICKS
        scaled = distance.astype(jnp.float32) / TICKS
        shaped = sinc(scaled) * sinc(scaled / 3.0)
        pieces.append(jnp.where(inside, shaped, jnp.zeros_like(shaped)))
    table = jnp.concatenate(pieces, axis=0).astype(jnp.bfloat16)
    inner = table[:, :tok_dev]
    outer = table[:, tok_dev:tok_dev + 2 * halo]

    @pl.when(me > 0)
    def _():
        upward(me - 1).wait_recv()

    @pl.when(me < devices - 1)
    def _():
        downward(me + 1).wait_recv()

    def columns(index):
        return pl.ds(pl.multiple_of(index * slab, slab), slab)

    def rows(index):
        return pl.ds(pl.multiple_of(index * 16, 16), 16)

    def give(group, index):
        return pltpu.make_async_remote_copy(
            src_ref=held.at[rows(group), columns(index)], dst_ref=out_ref.at[rows(me), :],
            send_sem=send_x.at[group * vox + index], recv_sem=recv_x.at[me],
            device_id={"subj": group, "vox": index}, device_id_type=MESH,
        )

    def taken(source):
        return pltpu.make_async_remote_copy(
            src_ref=held.at[rows(0), columns(0)], dst_ref=out_ref.at[rows(source), :],
            send_sem=send_x.at[source], recv_sem=recv_x.at[source],
            device_id=place(source), device_id_type=MESH,
        )

    def make(index):
        summed = jnp.dot(inner, feat_ref[:, columns(index)], preferred_element_type=jnp.float32)
        summed = summed + jnp.dot(
            outer, edges[:, columns(index)], preferred_element_type=jnp.float32
        )
        held[:, columns(index)] = (summed * scale).astype(jnp.bfloat16)

    @pl.loop(1, vox)
    def _(step):
        index = lax.rem(my_vox + step, vox)
        make(index)
        for turn in range(groups):
            give(lax.rem(my_group + turn, groups), index).start()

    make(my_vox)
    for turn in range(1, groups):
        give(lax.rem(my_group + turn, groups), my_vox).start()
    out_ref[rows(me), :] = held[rows(my_group), columns(my_vox)]

    @pl.loop(1, devices)
    def _(turn):
        other = lax.rem(me + turn, devices)
        taken(other).wait_recv()

    @pl.loop(1, devices)
    def _(turn):
        other = lax.rem(me + turn, devices)
        give(other // vox, lax.rem(other, vox)).wait_send()

    if share:
        for turn in range(1, chips):
            lent(turn).wait_recv()
        for turn in range(1, chips):
            lend(turn).wait_send()

    for turn in range(1, groups):
        tell(turn).wait_send()

    @pl.when(me < devices - 1)
    def _():
        upward(me + 1).wait_send()

    @pl.when(me > 0)
    def _():
        downward(me - 1).wait_send()


def spread_interp(features, ticks, shift, targets, share, groups, vox, rows_dev, halo):
    tok_dev, width = features.shape
    devices = groups * vox
    slab = width // vox
    lanes = ticks.shape[1]
    return pl.pallas_call(
        functools.partial(
            spread_kernel, groups, vox, rows_dev, (GAP / TICKS) ** 0.5, share
        ),
        out_shape=[
            jax.ShapeDtypeStruct((devices * 16, slab), jnp.bfloat16),
            jax.ShapeDtypeStruct((vox // 2, *targets.shape), jnp.float32),
        ],
        in_specs=[pl.BlockSpec(memory_space=pltpu.VMEM)] * 4,
        out_specs=[pl.BlockSpec(memory_space=pltpu.VMEM)] * 2,
        scratch_shapes=[
            pltpu.VMEM((2 * halo, width), jnp.bfloat16),
            pltpu.VMEM((groups, 8, lanes), jnp.int32),
            pltpu.VMEM((groups * 16, width), jnp.bfloat16),
            pltpu.SemaphoreType.DMA((groups,)),
            pltpu.SemaphoreType.DMA((groups,)),
            pltpu.SemaphoreType.DMA((2,)),
            pltpu.SemaphoreType.DMA((2,)),
            pltpu.SemaphoreType.DMA((devices,)),
            pltpu.SemaphoreType.DMA((devices,)),
            pltpu.SemaphoreType.DMA((vox // 2,)),
            pltpu.SemaphoreType.DMA((vox // 2,)),
        ],
        compiler_params=pltpu.CompilerParams(
            collective_id=1, has_side_effects=True, vmem_limit_bytes=32 * 2**20
        ),
        name="spread_interp",
    )(features, ticks, shift, targets)


def gram_kernel(n, scale, share, stacked_ref, half_ref, out_ref, other_ref, part, land,
                send_a, recv_a, send_b, recv_b, pair_sem):
    me = lax.axis_index("vox")
    blocks = stacked_ref.shape[0] // BLOCK
    rows = out_ref.shape[0] // n
    barrier = pltpu.get_barrier_semaphore()
    for step in range(1, n):
        pl.semaphore_signal(
            barrier, inc=1, device_id={"vox": lax.rem(me + step, n)}, device_id_type=MESH
        )

    def fill(i, j):
        def tall(index):
            start = index * BLOCK
            return pl.ds(start if isinstance(start, int) else pl.multiple_of(start, BLOCK), BLOCK)

        part[tall(i * (i + 1) // 2 + j), :] = lax.dot_general(
            stacked_ref[tall(i), :], stacked_ref[tall(j), :], (((1,), (1,)), ((), ())),
            preferred_element_type=jnp.float32,
        )

    if blocks <= 4:
        for i in range(blocks):
            for j in range(i + 1):
                fill(i, j)
    else:

        @pl.loop(0, blocks)
        def _(i):
            @pl.loop(0, i + 1)
            def _(j):
                fill(i, j)

    pl.semaphore_wait(barrier, n - 1)
    hand = pltpu.make_async_remote_copy(
        src_ref=half_ref, dst_ref=other_ref, send_sem=pair_sem.at[0], recv_sem=pair_sem.at[1],
        device_id={"vox": me + 1 - 2 * lax.rem(me, 2)}, device_id_type=MESH,
    )

    def rows_of(owner):
        return pl.ds(pl.multiple_of(owner * rows, rows), rows)

    def share(step):
        peer = lax.rem(me + step, n)
        return pltpu.make_async_remote_copy(
            src_ref=part.at[rows_of(peer), :], dst_ref=land.at[me],
            send_sem=send_a.at[step], recv_sem=recv_a.at[me],
            device_id={"vox": peer}, device_id_type=MESH,
        )

    def arrived(step):
        peer = lax.rem(me + step, n)
        return pltpu.make_async_remote_copy(
            src_ref=part.at[rows_of(me), :], dst_ref=land.at[peer],
            send_sem=send_a.at[step], recv_sem=recv_a.at[peer],
            device_id={"vox": peer}, device_id_type=MESH,
        )

    def spread(step):
        peer = lax.rem(me + step, n)
        return pltpu.make_async_remote_copy(
            src_ref=out_ref.at[rows_of(me), :], dst_ref=out_ref.at[rows_of(me), :],
            send_sem=send_b.at[step], recv_sem=recv_b.at[me],
            device_id={"vox": peer}, device_id_type=MESH,
        )

    def spread_in(step):
        peer = lax.rem(me + step, n)
        return pltpu.make_async_remote_copy(
            src_ref=out_ref.at[rows_of(peer), :], dst_ref=out_ref.at[rows_of(peer), :],
            send_sem=send_b.at[step], recv_sem=recv_b.at[peer],
            device_id={"vox": peer}, device_id_type=MESH,
        )

    for step in range(1, n):
        share(step).start()
    total_rows = part[rows_of(me), :]
    for step in range(1, n):
        arrived(step).wait_recv()
        total_rows = total_rows + land[lax.rem(me + step, n)]
    out_ref[rows_of(me), :] = total_rows * scale
    for step in range(1, n):
        spread(step).start()
    if share:
        hand.start()
    for step in range(1, n):
        spread_in(step).wait_recv()
    if share:
        hand.wait()
    for step in range(1, n):
        share(step).wait_send()
        spread(step).wait_send()


def gram_sum(stacked, half, share, n, width):
    blocks = stacked.shape[0] // BLOCK
    tall = blocks * (blocks + 1) // 2 * BLOCK
    block = pl.BlockSpec(memory_space=pltpu.VMEM)
    return pl.pallas_call(
        functools.partial(gram_kernel, n, 1.0 / (DELAYS * width), share),
        out_shape=[
            jax.ShapeDtypeStruct((tall, BLOCK), jnp.float32),
            jax.ShapeDtypeStruct(half.shape, jnp.float32),
        ],
        in_specs=[block, block],
        out_specs=[block, block],
        scratch_shapes=[
            pltpu.VMEM((tall, BLOCK), jnp.float32),
            pltpu.VMEM((n, tall // n, BLOCK), jnp.float32),
            pltpu.SemaphoreType.DMA((n,)),
            pltpu.SemaphoreType.DMA((n,)),
            pltpu.SemaphoreType.DMA((n,)),
            pltpu.SemaphoreType.DMA((n,)),
            pltpu.SemaphoreType.DMA((2,)),
        ],
        compiler_params=pltpu.CompilerParams(
            collective_id=0, has_side_effects=True, vmem_limit_bytes=48 * 2**20
        ),
        name="gram_sum",
    )(stacked, half)


def full_dot(a, b):
    return jnp.dot(a, b, precision=FULL, preferred_element_type=jnp.float32)


def ridge(work, pair, total, penalty):
    blocks = total // BLOCK
    row = lax.broadcasted_iota(jnp.int32, (BLOCK, BLOCK), 0)
    col = lax.broadcasted_iota(jnp.int32, (BLOCK, BLOCK), 1)
    eye = jnp.where(row == col, 1.0, 0.0).astype(jnp.float32)
    for k in range(blocks):
        here = slice(k * BLOCK, (k + 1) * BLOCK)
        work[here, here] = work[here, here] + penalty * eye
    low = penalty * 0.9
    for k in range(blocks):
        here = slice(k * BLOCK, (k + 1) * BLOCK)
        after = (k + 1) * BLOCK
        diagonal = work[here, here]
        high = jnp.max(jnp.sum(jnp.abs(diagonal), axis=1))
        first = 2.0 / (low + high)
        pair[:BLOCK] = first * eye
        pair[BLOCK:] = first * diagonal

        def going(least):
            return least < 1.0 - 2.0**-12

        def step(least):
            inner = least * (2.0 - least)
            grow = 2.0 / (1.0 + inner)
            pair[...] = full_dot(pair[...], grow * (2.0 * eye - pair[BLOCK:]))
            return inner * grow

        lax.while_loop(going, step, low * first)
        inverse = pair[:BLOCK]
        inverse = inverse + full_dot(inverse, eye - full_dot(diagonal, inverse))
        ahead = full_dot(inverse, work[here, after:])
        work[here, after:] = ahead
        rest = blocks - 1 - k
        if 0 < rest <= 2:
            work[after:total, after:] -= full_dot(work[after:total, here], ahead)
        elif rest:

            @pl.loop(k + 1, blocks)
            def _(below):
                there = pl.ds(pl.multiple_of(below * BLOCK, BLOCK), BLOCK)
                work[there, after:] -= full_dot(work[there, here], work[here, after:])

    for k in range(blocks - 2, -1, -1):
        here = slice(k * BLOCK, (k + 1) * BLOCK)
        after = (k + 1) * BLOCK
        if blocks - 1 - k <= 2:
            work[here, total:] -= full_dot(work[here, after:total], work[after:total, total:])
        else:
            for below in range(k + 1, blocks):
                there = slice(below * BLOCK, (below + 1) * BLOCK)
                work[here, total:] -= full_dot(work[here, there], work[there, total:])


def unfold(kernel_ref, work, total):
    for i in range(total // BLOCK):
        rows = slice(i * BLOCK, (i + 1) * BLOCK)
        for j in range(i + 1):
            columns = slice(j * BLOCK, (j + 1) * BLOCK)
            start = (i * (i + 1) // 2 + j) * BLOCK
            block = kernel_ref[start:start + BLOCK, :]
            work[rows, columns] = block
            if j < i:
                work[columns, rows] = block.T


def dual_kernel(kernel_ref, penalty_ref, targets_ref, out_ref, work, pair):
    total = targets_ref.shape[0]
    unfold(kernel_ref, work, total)
    work[:, total:] = targets_ref[...]
    ridge(work, pair, total, penalty_ref[0])
    out_ref[...] = work[:, total:].astype(out_ref.dtype)


def solve_kernel(scale, kernel_ref, penalty_ref, half_ref, other_ref, stacked_ref, out_ref,
                 work, pair, dual, result, done, fetched):
    chips, total, voxels = half_ref.shape
    core = lax.rem(lax.axis_index("vox"), 2)
    fetches = []
    for chip in range(chips):
        for source, side in ((half_ref, core), (other_ref, 1 - core)):
            start = pl.multiple_of(total + (2 * chip + side) * voxels, BLOCK)
            fetches.append(
                pltpu.make_async_copy(
                    source.at[chip], work.at[:, pl.ds(start, voxels)], fetched.at[len(fetches)]
                )
            )
    for fetch in fetches:
        fetch.start()
    unfold(kernel_ref, work, total)
    for fetch in fetches:
        fetch.wait()
    ridge(work, pair, total, penalty_ref[0])
    dual[...] = work[:, total:].astype(dual.dtype)
    slab = result.shape[1]

    def leave(step):
        return pltpu.make_async_copy(result.at[step], out_ref.at[0, step], done.at[step])

    for step in range(DELAYS):
        projected = lax.dot_general(
            stacked_ref[:, step * slab:(step + 1) * slab], dual[...], (((0,), (0,)), ((), ())),
            preferred_element_type=jnp.float32,
        )
        result[step] = (projected * scale).astype(result.dtype)
        leave(step).start()
    for step in range(DELAYS):
        leave(step).wait()


def solve_dual(kernel, penalty, targets):
    total, voxels = targets.shape
    block = pl.BlockSpec(memory_space=pltpu.VMEM)
    return pl.pallas_call(
        dual_kernel,
        out_shape=jax.ShapeDtypeStruct((total, voxels), jnp.bfloat16),
        in_specs=[block, pl.BlockSpec(memory_space=pltpu.SMEM), block],
        out_specs=pl.BlockSpec(memory_space=pltpu.VMEM),
        scratch_shapes=[
            pltpu.VMEM((total, total + voxels), jnp.float32),
            pltpu.VMEM((2 * BLOCK, BLOCK), jnp.float32),
        ],
        compiler_params=pltpu.CompilerParams(vmem_limit_bytes=48 * 2**20),
        name="ridge_dual",
    )(kernel, penalty, targets)


def solve(kernel, penalty, half, other, stacked, width):
    chips, total, voxels = half.shape
    parts = 2 * chips
    slab = stacked.shape[1] // DELAYS
    block = pl.BlockSpec(memory_space=pltpu.VMEM)
    away = pl.BlockSpec(memory_space=pl.ANY)
    return pl.pallas_call(
        functools.partial(solve_kernel, (DELAYS * width) ** (-0.5)),
        out_shape=jax.ShapeDtypeStruct((1, DELAYS, slab, parts * voxels), jnp.bfloat16),
        in_specs=[block, pl.BlockSpec(memory_space=pltpu.SMEM), away, away, block],
        out_specs=pl.BlockSpec(memory_space=pl.ANY),
        scratch_shapes=[
            pltpu.VMEM((total, total + parts * voxels), jnp.float32),
            pltpu.VMEM((2 * BLOCK, BLOCK), jnp.float32),
            pltpu.VMEM((total, parts * voxels), jnp.bfloat16),
            pltpu.VMEM((DELAYS, slab, parts * voxels), jnp.bfloat16),
            pltpu.SemaphoreType.DMA((DELAYS,)),
            pltpu.SemaphoreType.DMA((parts,)),
        ],
        compiler_params=pltpu.CompilerParams(vmem_limit_bytes=60 * 2**20),
        name="ridge_solve",
    )(kernel, penalty, half, other, stacked)


def body(features, token_ticks, offsets, run_lengths, penalty, responses):
    tok_dev, width = features.shape
    group_count = lax.axis_size("subj")
    vox_count = lax.axis_size("vox")
    devices = group_count * vox_count
    slab_width = width // vox_count
    rows_dev = tok_dev * GAP // TICKS
    tr_total = rows_dev * devices
    halo = 3 * TICKS // GAP
    me = lax.axis_index("subj") * vox_count + lax.axis_index("vox")
    whole = tr_total <= 4 * BLOCK
    targets = responses[0] if whole else responses[0, :8]

    far = jnp.full((tok_dev,), -(2**20), jnp.int32)
    padded = jnp.concatenate([far, token_ticks, far])
    near = lax.dynamic_slice_in_dim(padded, me * tok_dev + tok_dev - halo, tok_dev + 2 * halo, 0)
    ticks = jnp.concatenate(
        [near[halo:halo + tok_dev], near[:halo], near[halo + tok_dev:], far[:tok_dev - 2 * halo]]
    )
    ticks = jnp.broadcast_to(ticks, (8, 2 * tok_dev))
    shift = jnp.broadcast_to(offsets[0], (8, 2 * tok_dev))
    blocks, half = spread_interp(
        features, ticks, shift, targets, whole, group_count, vox_count, rows_dev, halo
    )
    interp = blocks.reshape(devices, 16, slab_width)[:, :rows_dev].reshape(tr_total, slab_width)

    stacked = delay_stack(interp, run_lengths[0], tr_total)
    kernel, other = gram_sum(stacked, half, whole, vox_count, width)
    if whole:
        return solve(kernel, penalty, half, other, stacked, width)
    dual_coef = solve_dual(kernel, penalty, responses[0])
    projected = lax.dot_general(
        stacked,
        lax.all_gather(dual_coef, "vox", axis=1, tiled=True),
        (((0,), (0,)), ((), ())),
        preferred_element_type=jnp.float32,
    )
    projected = (projected * (DELAYS * width) ** (-0.5)).astype(jnp.bfloat16)
    return projected.reshape(1, DELAYS, slab_width, projected.shape[1])


def solution(mesh):
    return jax.shard_map(
        body,
        mesh=mesh,
        in_specs=(
            P(("subj", "vox"), None),
            P(),
            P("subj"),
            P("subj", None),
            P("subj"),
            P("subj", None, "vox"),
        ),
        out_specs=P("subj", None, "vox", None),
        check_vma=False,
    )
```

```python
import functools

import jax
import jax.numpy as jnp
from jax import lax
from jax.experimental import pallas as pl
from jax.experimental.pallas import tpu as pltpu
from jax.sharding import PartitionSpec as P

DELAYS = 4
TICKS = 64
GAP = 6
BLOCK = 128
FULL = lax.Precision.HIGHEST
MESH = pl.DeviceIdType.MESH


def delay_stack(interp, lengths, tr_total):
    runs = jnp.arange(lengths.shape[0])
    starts = jnp.sum(jnp.where(runs[None, :] < runs[:, None], lengths[None, :], 0), axis=1)
    tr_steps = jnp.arange(tr_total, dtype=jnp.int32)
    run_first = jnp.max(jnp.where(starts[None, :] <= tr_steps[:, None], starts[None, :], 0), axis=1)
    delayed = []
    for delay_step in range(1, DELAYS + 1):
        moved = jnp.concatenate(
            [jnp.zeros((delay_step, interp.shape[1]), interp.dtype), interp[:-delay_step]], axis=0
        )
        keep_rows = (tr_steps - delay_step >= run_first)[:, None]
        delayed.append(jnp.where(keep_rows, moved, jnp.zeros_like(moved)))
    return jnp.concatenate(delayed, axis=1)


def sinc(x):
    angle = jnp.pi * x
    return jnp.where(x == 0, 1.0, jnp.sin(angle) / jnp.where(x == 0, 1.0, angle))


def spread_kernel(groups, vox, rows_dev, scale, share, store_ref, tick_ref, shift_ref, target_ref,
                  out_ref, half_ref, edges, shifts, held, send_o, recv_o, send_e, recv_e,
                  send_x, recv_x, send_r, recv_r, feat_ref, near_sem):
    tok_dev, width = feat_ref.shape
    slab = width // vox
    halo = edges.shape[0] // 2
    devices = groups * vox
    my_group = lax.axis_index("subj")
    my_vox = lax.axis_index("vox")
    me = my_group * vox + my_vox

    def place(device):
        return {"subj": device // vox, "vox": lax.rem(device, vox)}

    barrier = pltpu.get_barrier_semaphore()

    @pl.loop(1, devices)
    def _(turn):
        pl.semaphore_signal(
            barrier, inc=1, device_id=place(lax.rem(me + turn, devices)), device_id_type=MESH
        )

    fetch = pltpu.make_async_copy(store_ref, feat_ref, near_sem.at[0])
    fetch.start()
    keep = pltpu.make_async_copy(target_ref, half_ref.at[my_vox // 2], near_sem.at[1])
    if share:
        keep.start()
    shifts[my_group] = shift_ref[...]
    pl.semaphore_wait(barrier, devices - 1)

    def tell(turn):
        return pltpu.make_async_remote_copy(
            src_ref=shift_ref, dst_ref=shifts.at[my_group],
            send_sem=send_o.at[turn], recv_sem=recv_o.at[my_group],
            device_id={"subj": lax.rem(my_group + turn, groups)}, device_id_type=MESH,
        )

    def told(turn):
        other = lax.rem(my_group + turn, groups)
        return pltpu.make_async_remote_copy(
            src_ref=shift_ref, dst_ref=shifts.at[other],
            send_sem=send_o.at[turn], recv_sem=recv_o.at[other],
            device_id={"subj": other}, device_id_type=MESH,
        )

    def upward(peer):
        return pltpu.make_async_remote_copy(
            src_ref=store_ref.at[tok_dev - halo:, :], dst_ref=edges.at[:halo, :],
            send_sem=send_e.at[0], recv_sem=recv_e.at[0],
            device_id=place(peer), device_id_type=MESH,
        )

    def downward(peer):
        return pltpu.make_async_remote_copy(
            src_ref=store_ref.at[:halo, :], dst_ref=edges.at[halo:, :],
            send_sem=send_e.at[1], recv_sem=recv_e.at[1],
            device_id=place(peer), device_id_type=MESH,
        )

    chips = vox // 2
    chip, core = my_vox // 2, lax.rem(my_vox, 2)

    def lend(turn):
        other = lax.rem(chip + turn, chips)
        return pltpu.make_async_remote_copy(
            src_ref=target_ref, dst_ref=half_ref.at[chip],
            send_sem=send_r.at[turn], recv_sem=recv_r.at[chip],
            device_id={"vox": other * 2 + core}, device_id_type=MESH,
        )

    def lent(turn):
        other = lax.rem(chip + turn, chips)
        return pltpu.make_async_remote_copy(
            src_ref=target_ref, dst_ref=half_ref.at[other],
            send_sem=send_r.at[turn], recv_sem=recv_r.at[other],
            device_id={"vox": other * 2 + core}, device_id_type=MESH,
        )

    for turn in range(1, groups):
        tell(turn).start()

    @pl.when(me < devices - 1)
    def _():
        upward(me + 1).start()

    @pl.when(me > 0)
    def _():
        downward(me - 1).start()

    @pl.when(me == 0)
    def _():
        edges[:halo, :] = jnp.zeros((halo, width), edges.dtype)

    @pl.when(me == devices - 1)
    def _():
        edges[halo:, :] = jnp.zeros((halo, width), edges.dtype)

    for turn in range(1, groups):
        told(turn).wait_recv()
    near = tick_ref[0:1, :]
    first = (me * rows_dev + lax.broadcasted_iota(jnp.int32, (16, near.shape[1]), 0)) * TICKS
    pieces = []
    for group in range(groups):
        distance = near - (first + shifts[group][0:1, :])
        inside = jnp.abs(distance) < 3 * TICKS
        scaled = distance.astype(jnp.float32) / TICKS
        shaped = sinc(scaled) * sinc(scaled / 3.0)
        pieces.append(jnp.where(inside, shaped, jnp.zeros_like(shaped)))
    table = jnp.concatenate(pieces, axis=0).astype(jnp.bfloat16)
    fetch.wait()
    inner = table[:, :tok_dev]
    outer = table[:, tok_dev:tok_dev + 2 * halo]

    @pl.when(me > 0)
    def _():
        upward(me - 1).wait_recv()

    @pl.when(me < devices - 1)
    def _():
        downward(me + 1).wait_recv()

    def columns(index):
        return pl.ds(pl.multiple_of(index * slab, slab), slab)

    def rows(index):
        return pl.ds(pl.multiple_of(index * 16, 16), 16)

    def give(group, index):
        return pltpu.make_async_remote_copy(
            src_ref=held.at[rows(group), columns(index)], dst_ref=out_ref.at[rows(me), :],
            send_sem=send_x.at[group * vox + index], recv_sem=recv_x.at[me],
            device_id={"subj": group, "vox": index}, device_id_type=MESH,
        )

    def taken(source):
        return pltpu.make_async_remote_copy(
            src_ref=held.at[rows(0), columns(0)], dst_ref=out_ref.at[rows(source), :],
            send_sem=send_x.at[source], recv_sem=recv_x.at[source],
            device_id=place(source), device_id_type=MESH,
        )

    def make(index):
        summed = jnp.dot(inner, feat_ref[:, columns(index)], preferred_element_type=jnp.float32)
        summed = summed + jnp.dot(
            outer, edges[:, columns(index)], preferred_element_type=jnp.float32
        )
        held[:, columns(index)] = (summed * scale).astype(jnp.bfloat16)

    @pl.loop(1, vox)
    def _(step):
        index = lax.rem(my_vox + step, vox)
        make(index)
        for turn in range(groups):
            give(lax.rem(my_group + turn, groups), index).start()

    if share:
        for turn in range(1, chips):
            lend(turn).start()

    make(my_vox)
    for turn in range(1, groups):
        give(lax.rem(my_group + turn, groups), my_vox).start()
    out_ref[rows(me), :] = held[rows(my_group), columns(my_vox)]

    @pl.loop(1, devices)
    def _(turn):
        other = lax.rem(me + turn, devices)
        taken(other).wait_recv()

    @pl.loop(1, devices)
    def _(turn):
        other = lax.rem(me + turn, devices)
        give(other // vox, lax.rem(other, vox)).wait_send()

    if share:
        keep.wait()
        for turn in range(1, chips):
            lent(turn).wait_recv()
        for turn in range(1, chips):
            lend(turn).wait_send()

    for turn in range(1, groups):
        tell(turn).wait_send()

    @pl.when(me < devices - 1)
    def _():
        upward(me + 1).wait_send()

    @pl.when(me > 0)
    def _():
        downward(me - 1).wait_send()


def spread_interp(features, ticks, shift, targets, share, groups, vox, rows_dev, halo):
    tok_dev, width = features.shape
    devices = groups * vox
    slab = width // vox
    lanes = ticks.shape[1]
    block = pl.BlockSpec(memory_space=pltpu.VMEM)
    far = pl.BlockSpec(memory_space=pltpu.HBM)
    return pl.pallas_call(
        functools.partial(
            spread_kernel, groups, vox, rows_dev, (GAP / TICKS) ** 0.5, share
        ),
        out_shape=[
            jax.ShapeDtypeStruct((devices * 16, slab), jnp.bfloat16),
            jax.ShapeDtypeStruct((vox // 2, *targets.shape), jnp.float32),
        ],
        in_specs=[far, block, block, far],
        out_specs=[block, far],
        scratch_shapes=[
            pltpu.VMEM((2 * halo, width), jnp.bfloat16),
            pltpu.VMEM((groups, 8, lanes), jnp.int32),
            pltpu.VMEM((groups * 16, width), jnp.bfloat16),
            pltpu.SemaphoreType.DMA((groups,)),
            pltpu.SemaphoreType.DMA((groups,)),
            pltpu.SemaphoreType.DMA((2,)),
            pltpu.SemaphoreType.DMA((2,)),
            pltpu.SemaphoreType.DMA((devices,)),
            pltpu.SemaphoreType.DMA((devices,)),
            pltpu.SemaphoreType.DMA((vox // 2,)),
            pltpu.SemaphoreType.DMA((vox // 2,)),
            pltpu.VMEM((tok_dev, width), jnp.bfloat16),
            pltpu.SemaphoreType.DMA((2,)),
        ],
        compiler_params=pltpu.CompilerParams(
            collective_id=1, has_side_effects=True, vmem_limit_bytes=61 * 2**20
        ),
        name="spread_interp",
    )(features, ticks, shift, targets)


def gram_kernel(n, scale, share, stacked_ref, half_ref, out_ref, other_ref, part, land,
                send_a, recv_a, send_b, recv_b, pair_sem):
    me = lax.axis_index("vox")
    blocks = stacked_ref.shape[0] // BLOCK
    rows = out_ref.shape[0] // n
    barrier = pltpu.get_barrier_semaphore()
    for step in range(1, n):
        pl.semaphore_signal(
            barrier, inc=1, device_id={"vox": lax.rem(me + step, n)}, device_id_type=MESH
        )

    def fill(i, j):
        def tall(index):
            start = index * BLOCK
            return pl.ds(start if isinstance(start, int) else pl.multiple_of(start, BLOCK), BLOCK)

        part[tall(i * (i + 1) // 2 + j), :] = lax.dot_general(
            stacked_ref[tall(i), :], stacked_ref[tall(j), :], (((1,), (1,)), ((), ())),
            preferred_element_type=jnp.float32,
        )

    if blocks <= 4:
        for i in range(blocks):
            for j in range(i + 1):
                fill(i, j)
    else:

        @pl.loop(0, blocks)
        def _(i):
            @pl.loop(0, i + 1)
            def _(j):
                fill(i, j)

    pl.semaphore_wait(barrier, n - 1)
    hand = pltpu.make_async_remote_copy(
        src_ref=half_ref, dst_ref=other_ref, send_sem=pair_sem.at[0], recv_sem=pair_sem.at[1],
        device_id={"vox": me + 1 - 2 * lax.rem(me, 2)}, device_id_type=MESH,
    )

    def rows_of(owner):
        return pl.ds(pl.multiple_of(owner * rows, rows), rows)

    def share(step):
        peer = lax.rem(me + step, n)
        return pltpu.make_async_remote_copy(
            src_ref=part.at[rows_of(peer), :], dst_ref=land.at[me],
            send_sem=send_a.at[step], recv_sem=recv_a.at[me],
            device_id={"vox": peer}, device_id_type=MESH,
        )

    def arrived(step):
        peer = lax.rem(me + step, n)
        return pltpu.make_async_remote_copy(
            src_ref=part.at[rows_of(me), :], dst_ref=land.at[peer],
            send_sem=send_a.at[step], recv_sem=recv_a.at[peer],
            device_id={"vox": peer}, device_id_type=MESH,
        )

    def spread(step):
        peer = lax.rem(me + step, n)
        return pltpu.make_async_remote_copy(
            src_ref=out_ref.at[rows_of(me), :], dst_ref=out_ref.at[rows_of(me), :],
            send_sem=send_b.at[step], recv_sem=recv_b.at[me],
            device_id={"vox": peer}, device_id_type=MESH,
        )

    def spread_in(step):
        peer = lax.rem(me + step, n)
        return pltpu.make_async_remote_copy(
            src_ref=out_ref.at[rows_of(peer), :], dst_ref=out_ref.at[rows_of(peer), :],
            send_sem=send_b.at[step], recv_sem=recv_b.at[peer],
            device_id={"vox": peer}, device_id_type=MESH,
        )

    for step in range(1, n):
        share(step).start()
    total_rows = part[rows_of(me), :]
    for step in range(1, n):
        arrived(step).wait_recv()
        total_rows = total_rows + land[lax.rem(me + step, n)]
    out_ref[rows_of(me), :] = total_rows * scale
    for step in range(1, n):
        spread(step).start()
    if share:
        hand.start()
    for step in range(1, n):
        spread_in(step).wait_recv()
    if share:
        hand.wait()
    for step in range(1, n):
        share(step).wait_send()
        spread(step).wait_send()


def gram_sum(stacked, half, share, n, width):
    blocks = stacked.shape[0] // BLOCK
    tall = blocks * (blocks + 1) // 2 * BLOCK
    block = pl.BlockSpec(memory_space=pltpu.VMEM)
    far = pl.BlockSpec(memory_space=pltpu.HBM)
    return pl.pallas_call(
        functools.partial(gram_kernel, n, 1.0 / (DELAYS * width), share),
        out_shape=[
            jax.ShapeDtypeStruct((tall, BLOCK), jnp.float32),
            jax.ShapeDtypeStruct(half.shape, jnp.float32),
        ],
        in_specs=[block, far],
        out_specs=[block, far],
        scratch_shapes=[
            pltpu.VMEM((tall, BLOCK), jnp.float32),
            pltpu.VMEM((n, tall // n, BLOCK), jnp.float32),
            pltpu.SemaphoreType.DMA((n,)),
            pltpu.SemaphoreType.DMA((n,)),
            pltpu.SemaphoreType.DMA((n,)),
            pltpu.SemaphoreType.DMA((n,)),
            pltpu.SemaphoreType.DMA((2,)),
        ],
        compiler_params=pltpu.CompilerParams(
            collective_id=0, has_side_effects=True, vmem_limit_bytes=48 * 2**20
        ),
        name="gram_sum",
    )(stacked, half)


def full_dot(a, b):
    return jnp.dot(a, b, precision=FULL, preferred_element_type=jnp.float32)


def ridge(work, pair, total, penalty):
    blocks = total // BLOCK
    row = lax.broadcasted_iota(jnp.int32, (BLOCK, BLOCK), 0)
    col = lax.broadcasted_iota(jnp.int32, (BLOCK, BLOCK), 1)
    eye = jnp.where(row == col, 1.0, 0.0).astype(jnp.float32)
    for k in range(blocks):
        here = slice(k * BLOCK, (k + 1) * BLOCK)
        work[here, here] = work[here, here] + penalty * eye
    low = penalty * 0.9
    for k in range(blocks):
        here = slice(k * BLOCK, (k + 1) * BLOCK)
        after = (k + 1) * BLOCK
        diagonal = work[here, here]
        high = jnp.max(jnp.sum(jnp.abs(diagonal), axis=1))
        first = 2.0 / (low + high)
        pair[:BLOCK] = first * eye
        pair[BLOCK:] = first * diagonal

        def going(least):
            return least < 1.0 - 2.0**-12

        def step(least):
            inner = least * (2.0 - least)
            grow = 2.0 / (1.0 + inner)
            pair[...] = full_dot(pair[...], grow * (2.0 * eye - pair[BLOCK:]))
            return inner * grow

        lax.while_loop(going, step, low * first)
        inverse = pair[:BLOCK]
        inverse = inverse + full_dot(inverse, eye - full_dot(diagonal, inverse))
        ahead = full_dot(inverse, work[here, after:])
        work[here, after:] = ahead
        rest = blocks - 1 - k
        if 0 < rest <= 2:
            work[after:total, after:] -= full_dot(work[after:total, here], ahead)
        elif rest:

            @pl.loop(k + 1, blocks)
            def _(below):
                there = pl.ds(pl.multiple_of(below * BLOCK, BLOCK), BLOCK)
                work[there, after:] -= full_dot(work[there, here], work[here, after:])

    for k in range(blocks - 2, -1, -1):
        here = slice(k * BLOCK, (k + 1) * BLOCK)
        after = (k + 1) * BLOCK
        if blocks - 1 - k <= 2:
            work[here, total:] -= full_dot(work[here, after:total], work[after:total, total:])
        else:
            for below in range(k + 1, blocks):
                there = slice(below * BLOCK, (below + 1) * BLOCK)
                work[here, total:] -= full_dot(work[here, there], work[there, total:])


def unfold(kernel_ref, work, total):
    for i in range(total // BLOCK):
        rows = slice(i * BLOCK, (i + 1) * BLOCK)
        for j in range(i + 1):
            columns = slice(j * BLOCK, (j + 1) * BLOCK)
            start = (i * (i + 1) // 2 + j) * BLOCK
            block = kernel_ref[start:start + BLOCK, :]
            work[rows, columns] = block
            if j < i:
                work[columns, rows] = block.T


def dual_kernel(kernel_ref, penalty_ref, targets_ref, out_ref, work, pair):
    total = targets_ref.shape[0]
    unfold(kernel_ref, work, total)
    work[:, total:] = targets_ref[...]
    ridge(work, pair, total, penalty_ref[0])
    out_ref[...] = work[:, total:].astype(out_ref.dtype)


def solve_kernel(scale, kernel_ref, penalty_ref, half_ref, other_ref, stacked_ref, out_ref,
                 work, pair, dual, result, done, fetched):
    chips, total, voxels = half_ref.shape
    core = lax.rem(lax.axis_index("vox"), 2)
    fetches = []
    for chip in range(chips):
        for source, side in ((half_ref, core), (other_ref, 1 - core)):
            start = pl.multiple_of(total + (2 * chip + side) * voxels, BLOCK)
            fetches.append(
                pltpu.make_async_copy(
                    source.at[chip], work.at[:, pl.ds(start, voxels)], fetched.at[len(fetches)]
                )
            )
    for fetch in fetches:
        fetch.start()
    unfold(kernel_ref, work, total)
    for fetch in fetches:
        fetch.wait()
    ridge(work, pair, total, penalty_ref[0])
    dual[...] = work[:, total:].astype(dual.dtype)
    slab = result.shape[1]

    def leave(step):
        return pltpu.make_async_copy(result.at[step], out_ref.at[0, step], done.at[step])

    for step in range(DELAYS):
        projected = lax.dot_general(
            stacked_ref[:, step * slab:(step + 1) * slab], dual[...], (((0,), (0,)), ((), ())),
            preferred_element_type=jnp.float32,
        )
        result[step] = (projected * scale).astype(result.dtype)
        leave(step).start()
    for step in range(DELAYS):
        leave(step).wait()


def solve_dual(kernel, penalty, targets):
    total, voxels = targets.shape
    block = pl.BlockSpec(memory_space=pltpu.VMEM)
    return pl.pallas_call(
        dual_kernel,
        out_shape=jax.ShapeDtypeStruct((total, voxels), jnp.bfloat16),
        in_specs=[block, pl.BlockSpec(memory_space=pltpu.SMEM), block],
        out_specs=pl.BlockSpec(memory_space=pltpu.VMEM),
        scratch_shapes=[
            pltpu.VMEM((total, total + voxels), jnp.float32),
            pltpu.VMEM((2 * BLOCK, BLOCK), jnp.float32),
        ],
        compiler_params=pltpu.CompilerParams(vmem_limit_bytes=48 * 2**20),
        name="ridge_dual",
    )(kernel, penalty, targets)


def solve(kernel, penalty, half, other, stacked, width):
    chips, total, voxels = half.shape
    parts = 2 * chips
    slab = stacked.shape[1] // DELAYS
    block = pl.BlockSpec(memory_space=pltpu.VMEM)
    away = pl.BlockSpec(memory_space=pl.ANY)
    far = pl.BlockSpec(memory_space=pltpu.HBM)
    return pl.pallas_call(
        functools.partial(solve_kernel, (DELAYS * width) ** (-0.5)),
        out_shape=jax.ShapeDtypeStruct((1, DELAYS, slab, parts * voxels), jnp.bfloat16),
        in_specs=[block, pl.BlockSpec(memory_space=pltpu.SMEM), far, far, block],
        out_specs=pl.BlockSpec(memory_space=pl.ANY),
        scratch_shapes=[
            pltpu.VMEM((total, total + parts * voxels), jnp.float32),
            pltpu.VMEM((2 * BLOCK, BLOCK), jnp.float32),
            pltpu.VMEM((total, parts * voxels), jnp.bfloat16),
            pltpu.VMEM((DELAYS, slab, parts * voxels), jnp.bfloat16),
            pltpu.SemaphoreType.DMA((DELAYS,)),
            pltpu.SemaphoreType.DMA((parts,)),
        ],
        compiler_params=pltpu.CompilerParams(vmem_limit_bytes=24 * 2**20),
        name="ridge_solve",
    )(kernel, penalty, half, other, stacked)


def body(features, token_ticks, offsets, run_lengths, penalty, responses):
    tok_dev, width = features.shape
    group_count = lax.axis_size("subj")
    vox_count = lax.axis_size("vox")
    devices = group_count * vox_count
    slab_width = width // vox_count
    rows_dev = tok_dev * GAP // TICKS
    tr_total = rows_dev * devices
    halo = 3 * TICKS // GAP
    me = lax.axis_index("subj") * vox_count + lax.axis_index("vox")
    whole = tr_total <= 4 * BLOCK
    targets = responses[0] if whole else responses[0, :8]

    far = jnp.full((tok_dev,), -(2**20), jnp.int32)
    padded = jnp.concatenate([far, token_ticks, far])
    near = lax.dynamic_slice_in_dim(padded, me * tok_dev + tok_dev - halo, tok_dev + 2 * halo, 0)
    ticks = jnp.concatenate(
        [near[halo:halo + tok_dev], near[:halo], near[halo + tok_dev:], far[:tok_dev - 2 * halo]]
    )
    ticks = jnp.broadcast_to(ticks, (8, 2 * tok_dev))
    shift = jnp.broadcast_to(offsets[0], (8, 2 * tok_dev))
    blocks, half = spread_interp(
        features, ticks, shift, targets, whole, group_count, vox_count, rows_dev, halo
    )
    interp = blocks.reshape(devices, 16, slab_width)[:, :rows_dev].reshape(tr_total, slab_width)

    stacked = delay_stack(interp, run_lengths[0], tr_total)
    kernel, other = gram_sum(stacked, half, whole, vox_count, width)
    if whole:
        return solve(kernel, penalty, half, other, stacked, width)
    dual_coef = solve_dual(kernel, penalty, responses[0])
    projected = lax.dot_general(
        stacked,
        lax.all_gather(dual_coef, "vox", axis=1, tiled=True),
        (((0,), (0,)), ((), ())),
        preferred_element_type=jnp.float32,
    )
    projected = (projected * (DELAYS * width) ** (-0.5)).astype(jnp.bfloat16)
    return projected.reshape(1, DELAYS, slab_width, projected.shape[1])


def solution(mesh):
    return jax.shard_map(
        body,
        mesh=mesh,
        in_specs=(
            P(("subj", "vox"), None),
            P(),
            P("subj"),
            P("subj", None),
            P("subj"),
            P("subj", None, "vox"),
        ),
        out_specs=P("subj", None, "vox", None),
        check_vma=False,
    )
```
